32 devices in a mesh: ctx: 8 (over z, y), exp: 4 (over x, core).
Axes of the slice: x: 2, y: 2, z: 4, core: 2. Of those that a mesh axis runs over, the one named last changes fastest.
Arguments:
- inputs: bfloat16 [1024, 4096], P('ctx', 'exp'), may hold values from -6 to 6
- gate_input: bfloat16 [1024, 4096], P('ctx', 'exp')
- b_proj: bfloat16 [1024, 128], P('ctx'), may hold values from -0.5 to 0.5
- c_proj: bfloat16 [1024, 128], P('ctx'), may hold values from -6 to 6
- step_size: float32 [64, 1024], P('exp', 'ctx'), may hold values from 0.03 to 0.3
- decay_rate: float32 [64, 1024], P('exp', 'ctx'), as said below
- skip_gain: float32 [64], P('exp'), may hold values from 0.5 to 2
- start_state: float32 [64, 64, 128], P('exp'), may hold values from -3 to 3
- norm_gain: float32 [4096], P('exp'), may hold values from 0.5 to 1.5
- out_proj: bfloat16 [4096, 4096], P('exp', 'ctx'), may hold values from -0.09375 to 0.09375
- residual: bfloat16 [1024, 4096], P('ctx'), may hold values from -6 to 6
- moe_gain: float32 [4096], replicated, may hold values from 0.5 to 1.5
- w_gate: bfloat16 [8, 4096, 3584], P('ctx', None, 'exp'), may hold values from -0.09375 to 0.09375
- w_up: bfloat16 [8, 4096, 3584], P('ctx', None, 'exp'), may hold values from -0.09375 to 0.09375
- w_down: bfloat16 [8, 3584, 4096], P('ctx', 'exp'), may hold values from -0.0625 to 0.0625
- route_ids: int32 [1024, 2], P('ctx'), may hold values from 0 to 3, all different within a row; in each aligned block of 32 rows (0 to 31, 32 to 63, ...) at most 32 rows name the same one
- route_gates: float32 [1024, 2], P('ctx'), may hold values from 0.3 to 1
Outputs:
- output: bfloat16 [1024, 4096], P(('ctx', 'exp'))
The draws below stay inside these ranges and needn't reach their ends.
Inputs may be any that keep to these rules, and one draw needn't show every extreme that they name: `route_ids`: each row names two different experts. In each aligned block of 32 rows no expert is named more than 32 times, a bound that some block reaches. `decay_rate`: Non-negative.
All inputs are finite; a program needn't handle non-finite values.
Results may differ from the reference program's by a relative error of at most 0.02.
Values may be sent and summed in bfloat16 or wider, within the bound.
No kernel may reach another device: no remote copies, remote signals or barrier semaphores. Data moves between devices by JAX's collectives and lax.ppermute only.
A program may use at most 128 MiB of HBM per device.

```python
import math
import jax
import jax.numpy as jnp
import numpy as np
from jax import lax

D = 4096
RECURRENT_GROUPS = 64
P_SIZE = 64
N = 128
FF = 7168
PAIR = 2
TOK_CTX = 128
EXPERTS = 4
SPAN_ENTRIES = 1024
TOK_Q = 32
CAP = 32
N_EXP = 4


def draw_gate_input(key, part):
    stochastic_seeds = jax.random.split(key, 3)
    columns = RECURRENT_GROUPS * P_SIZE
    ramp = jnp.exp(jnp.log(3.0) * jnp.arange(columns, dtype=jnp.float32) / columns)
    column_scale = ramp * jnp.exp(jax.random.uniform(stochastic_seeds[0], (columns,), minval=0.0, maxval=jnp.log(10.0))) / 3.0
    row_scale = jnp.exp(jax.random.uniform(stochastic_seeds[1], (SPAN_ENTRIES, 1), minval=0.0, maxval=jnp.log(4.0)))
    noise = jax.random.normal(stochastic_seeds[2], (SPAN_ENTRIES, columns))
    return (noise * row_scale * column_scale[None, :]).astype(jnp.bfloat16)


def draw_decay_rate(key, part):
    stochastic_seeds = jax.random.split(key, 7)
    fast_share = 0.5
    fast_heads = jax.random.uniform(stochastic_seeds[0], (RECURRENT_GROUPS,)) < fast_share
    fast_rate = jax.random.uniform(stochastic_seeds[1], (RECURRENT_GROUPS,), minval=1.0 / 50.0, maxval=1.0 / 30.0)
    slow_rate = jax.random.uniform(stochastic_seeds[2], (RECURRENT_GROUPS,), minval=0.1, maxval=0.5) / SPAN_ENTRIES
    nominal_speed = jnp.where(fast_heads, fast_rate, slow_rate)
    blocks = SPAN_ENTRIES // TOK_CTX
    hardware_multiplier = jnp.exp(jax.random.uniform(stochastic_seeds[3], (RECURRENT_GROUPS, blocks), minval=jnp.log(0.5), maxval=jnp.log(2.0)))
    hardware_multiplier = jnp.repeat(hardware_multiplier, TOK_CTX, axis=1)
    perturb_magnitude = jnp.exp(jax.random.uniform(stochastic_seeds[4], (RECURRENT_GROUPS, SPAN_ENTRIES), minval=jnp.log(0.7), maxval=jnp.log(1.4)))
    spike_offset = jax.random.randint(stochastic_seeds[5], (RECURRENT_GROUPS, 3), 0, SPAN_ENTRIES)
    spike_duration = jax.random.uniform(stochastic_seeds[6], (RECURRENT_GROUPS, 3), minval=0.22, maxval=0.5)
    sequence_indices = jnp.arange(SPAN_ENTRIES, dtype=jnp.int32)
    spike_collection = jnp.sum(jnp.where(sequence_indices[None, None, :] == spike_offset[:, :, None], spike_duration[:, :, None], 0.0), axis=1)
    return (nominal_speed[:, None] * hardware_multiplier * perturb_magnitude + spike_collection).astype(jnp.float32)


def block_scale(rng, shape, cuts, smallest, top_value):
    factor_of, own = 1.0, jax.random.fold_in(rng, 6)
    for dim, parts in cuts:
        heights = jnp.exp(jax.random.uniform(jax.random.fold_in(own, dim), (parts,), jnp.float32, smallest / len(cuts), top_value / len(cuts)))
        factor_of = factor_of * jnp.repeat(heights, shape[dim] // parts).reshape([-1 if axis == dim else 1 for axis in range(len(shape))])
    return factor_of


def shared_out(key, own, number, rows, amount, top, reach, skew):
    sequence = jax.random.permutation(key, amount)
    crowded, ordinary = portions_of(amount, rows * top, reach, skew, True), portions_of(amount, rows * top, reach, skew, False)
    places = jnp.arange(amount)

    def named(sizes, offset_by):
        used = int((sizes > 0).sum())
        fixed = max(1, used // 4)
        shifted = fixed + (places - fixed + offset_by * (used - fixed)) % max(1, amount - fixed)
        return jnp.zeros((amount,), jnp.int32).at[sequence[jnp.where(places < fixed, places, shifted)]].set(jnp.asarray(sizes, jnp.int32))

    sizes = jnp.where(number % 4 == 0, named(crowded, number // 4), named(ordinary, number - number // 4 - 1))
    mixed = jax.random.permutation(jax.random.fold_in(own, 3), amount)
    giver, sink = mixed[0:amount // 2 * 2:2], mixed[1:amount // 2 * 2:2]
    margin = jnp.minimum(sizes[giver] - 1, reach - sizes[sink]) // 2
    margin = jnp.where((giver == sequence[0]) | (sink == sequence[0]) | (sizes[sink] == 0), 0, jnp.maximum(margin, 0))
    shifted = jax.random.randint(jax.random.fold_in(own, 4), (amount // 2,), 0, 1 << 20) % (margin + 1)
    sizes = sizes.at[giver].add(-shifted).at[sink].add(shifted)
    labels = jnp.searchsorted(jnp.cumsum(sizes), jnp.arange(rows * top), side="right").astype(jnp.int32)
    listing = labels.reshape(top, rows).T
    listing = listing[jax.random.permutation(jax.random.fold_in(own, 1), rows)]
    offset_by = jax.random.randint(jax.random.fold_in(own, 2), (rows, 1), 0, top)
    return jnp.take_along_axis(listing, (jnp.arange(top)[None, :] + offset_by) % top, axis=1)


def portions_of(count, total, reach, slope, full):
    weights = [(1 << 20) // math.isqrt(grade ** slope) + 1 for grade in range(1, count + 1)]
    largest = reach if full else min(reach, max(-(-total // count), total * weights[0] // sum(weights)))
    least = 1 if total - largest >= count - 1 else 0
    given, spare = [largest] + [least] * (count - 1), total - largest - least * (count - 1)
    while spare > 0:
        free = [i for i in range(1, count) if given[i] < largest] or [i for i in range(1, count) if given[i] < reach]
        pool, remaining = sum([weights[i] for i in free]), spare
        for i in free:
            more = min(reach - given[i], max(1, remaining * weights[i] // pool), spare)
            given[i] = given[i] + more
            spare = spare - more
    return np.array(given)


def normal_values(key, shape, scale, most, shards=(), held_as=jnp.bfloat16):
    drawn = scale * jax.random.normal(key, shape, jnp.float32)
    if shards:
        drawn = drawn * block_scale(key, shape, shards, -0.22, 0.18)
    return jnp.clip(drawn, -most, most).astype(held_as)


def setup_inputs(seed: int = 0) -> dict:
    splits = jax.random.split(jax.random.key(seed), 18)
    inputs = normal_values(splits[0], (SPAN_ENTRIES, RECURRENT_GROUPS * P_SIZE), 1.0, 6.0, ((0, 8), (1, 4)))
    gate_input = draw_gate_input(jax.random.fold_in(splits[17], 71), 0)
    b_proj = normal_values(splits[2], (SPAN_ENTRIES, N), N ** -0.5, 0.5, ((0, 8),))
    c_proj = normal_values(splits[3], (SPAN_ENTRIES, N), 1.0, 6.0, ((0, 8),))
    step_size = jnp.clip(jnp.exp(math.log(0.3) - 2.3025852 * jax.random.uniform(splits[4], (RECURRENT_GROUPS, SPAN_ENTRIES), jnp.float32) ** block_scale(splits[4], (RECURRENT_GROUPS, SPAN_ENTRIES), ((0, 4), (1, 8)), -0.2, 0.2)), 0.03, 0.3)
    decay_rate = draw_decay_rate(jax.random.fold_in(splits[17], 71), 0)
    skip_gain = jnp.clip(0.5 + 1.5 * jax.random.uniform(splits[6], (RECURRENT_GROUPS,), jnp.float32) ** block_scale(splits[6], (RECURRENT_GROUPS,), ((0, 4),), -0.2, 0.2), 0.5, 2.0)
    start_state = normal_values(splits[7], (RECURRENT_GROUPS, P_SIZE, N), 0.5, 3.0, ((0, 4),), jnp.float32)
    norm_gain = jnp.clip(1.0 + 0.1 * jax.random.normal(splits[8], (RECURRENT_GROUPS * P_SIZE,), jnp.float32), 0.5, 1.5)
    out_proj = normal_values(splits[9], (RECURRENT_GROUPS * P_SIZE, D), (RECURRENT_GROUPS * P_SIZE) ** -0.5, 0.09375, ((0, 4), (1, 8)))
    residual = normal_values(splits[10], (SPAN_ENTRIES, D), 1.0, 6.0, ((0, 8),))
    moe_gain = jnp.clip(1.0 + 0.1 * jax.random.normal(splits[11], (D,), jnp.float32), 0.5, 1.5)
    w_gate = normal_values(splits[12], (EXPERTS * PAIR, D, FF // PAIR), D ** -0.5, 0.09375, ((0, 8), (2, 4)))
    w_up = normal_values(splits[13], (EXPERTS * PAIR, D, FF // PAIR), D ** -0.5, 0.09375, ((0, 8), (2, 4)))
    w_down = normal_values(splits[14], (EXPERTS * PAIR, FF // PAIR, D), FF ** -0.5, 0.0625, ((0, 8), (1, 4)))
    route_ids_keys = jax.random.split(jax.random.fold_in(splits[15], 1), SPAN_ENTRIES // TOK_Q)
    route_ids_turns = jax.random.permutation(jax.random.fold_in(splits[15], 3), SPAN_ENTRIES // TOK_Q)
    route_ids = jax.vmap(lambda own, number: shared_out(jax.random.fold_in(splits[15], 2), own, number, TOK_Q, EXPERTS, 2, CAP, 2))(route_ids_keys, route_ids_turns).reshape((SPAN_ENTRIES, 2))
    route_gates = jnp.clip(0.3 + 0.7 * jax.random.uniform(splits[16], (SPAN_ENTRIES, 2), jnp.float32) ** block_scale(splits[16], (SPAN_ENTRIES, 2), ((0, 8),), -0.2, 0.2), 0.3, 1.0)
    return dict(inputs=inputs, gate_input=gate_input, b_proj=b_proj, c_proj=c_proj, step_size=step_size, decay_rate=decay_rate, skip_gain=skip_gain, start_state=start_state, norm_gain=norm_gain, out_proj=out_proj, residual=residual, moe_gain=moe_gain, w_gate=w_gate, w_up=w_up, w_down=w_down, route_ids=route_ids, route_gates=route_gates)


eps_norm = 1e-05
top_precision = lax.Precision.HIGHEST

def span_scan(carry_state, pieces):
    x_block, b_block, c_block, step_block, rate_block = pieces
    length = x_block.shape[0]
    cumulative = jnp.cumsum(rate_block, axis=1)
    span_total = cumulative[:, -1]
    sequence_indices = jnp.arange(length, dtype=jnp.int32)
    causal = sequence_indices[:, None] >= sequence_indices[None, :]
    spread = jnp.where(causal[None], cumulative[:, :, None] - cumulative[:, None, :], 0.0)
    scores = jnp.dot(c_block, b_block.T, precision=top_precision)
    mixing = jnp.where(causal[None], jnp.exp(-spread), 0.0) * scores[None] * step_block[:, None, :]
    inside_part = jnp.einsum('hts,shp->thp', mixing, x_block, precision=top_precision)
    carried = jnp.einsum('hpn,tn->thp', carry_state, c_block, precision=top_precision) * jnp.exp(-cumulative).T[:, :, None]
    ending = jnp.exp(-(span_total[:, None] - cumulative)) * step_block
    local_state = jnp.einsum('hs,shp,sn->hpn', ending, x_block, b_block, precision=top_precision)
    new_state = jnp.exp(-span_total)[:, None, None] * carry_state + local_state
    return (new_state, inside_part + carried)

def experts_apply(moe_in, w_gate, w_up, w_down, route_ids, route_gates):
    flat_ids = route_ids.reshape(-1).astype(jnp.int32)
    rows_most = SPAN_ENTRIES // TOK_Q * CAP
    piece_width = FF // (PAIR * N_EXP)

    def one_expert(accumulated, expert):
        route_order = jnp.argsort((flat_ids != expert).astype(jnp.int32), stable=True)[:rows_most].astype(jnp.int32)
        is_live = flat_ids[route_order] == expert
        routed = moe_in[route_order // 2]
        result = jnp.zeros((rows_most, D), jnp.float32)
        for half_index in range(PAIR):
            row_index = (expert * PAIR + half_index).astype(jnp.int32)
            gate_part = lax.dynamic_index_in_dim(w_gate, row_index, 0, keepdims=False)
            up_part = lax.dynamic_index_in_dim(w_up, row_index, 0, keepdims=False)
            down_part = lax.dynamic_index_in_dim(w_down, row_index, 0, keepdims=False)
            half_sum = jnp.zeros((rows_most, D), jnp.float32)
            for quarter in range(N_EXP):
                lower = quarter * piece_width
                upper = lower + piece_width
                gate_val = jnp.dot(routed, gate_part[:, lower:upper], preferred_element_type=jnp.float32)
                up_val = jnp.dot(routed, up_part[:, lower:upper], preferred_element_type=jnp.float32)
                hidden_piece = (jax.nn.silu(gate_val) * up_val).astype(jnp.bfloat16)
                product = jnp.dot(hidden_piece, down_part[lower:upper, :], preferred_element_type=jnp.float32)
                half_sum = half_sum + lax.optimization_barrier(product.astype(jnp.bfloat16)).astype(jnp.float32)
            result = result + lax.optimization_barrier(half_sum.astype(jnp.bfloat16)).astype(jnp.float32)
        accumulated = accumulated.at[route_order].add(jnp.where(is_live[:, None], result, 0.0))
        return (accumulated, None)
    start_value = jnp.zeros((2 * SPAN_ENTRIES, D), jnp.float32)
    totals, unused = lax.scan(one_expert, start_value, jnp.arange(EXPERTS, dtype=jnp.int32))
    return lax.optimization_barrier(jnp.sum(totals.reshape(SPAN_ENTRIES, 2, D) * route_gates[:, :, None].astype(jnp.float32), axis=1))

def reference(inputs, gate_input, b_proj, c_proj, step_size, decay_rate, skip_gain, start_state, norm_gain, out_proj, residual, moe_gain, w_gate, w_up, w_down, route_ids, route_gates):
    spans = SPAN_ENTRIES // TOK_CTX
    x_whole = inputs.astype(jnp.float32)
    x_all = x_whole.reshape(spans, TOK_CTX, RECURRENT_GROUPS, P_SIZE)
    b_all = b_proj.astype(jnp.float32).reshape(spans, TOK_CTX, N)
    c_all = c_proj.astype(jnp.float32).reshape(spans, TOK_CTX, N)
    step_all = step_size.reshape(RECURRENT_GROUPS, spans, TOK_CTX).transpose(1, 0, 2)
    rate_all = decay_rate.reshape(RECURRENT_GROUPS, spans, TOK_CTX).transpose(1, 0, 2)
    end_state, ssm_part = lax.scan(span_scan, start_state.astype(jnp.float32), (x_all, b_all, c_all, step_all, rate_all))
    ssm_out = ssm_part.reshape(SPAN_ENTRIES, RECURRENT_GROUPS, P_SIZE) + skip_gain[None, :, None] * x_whole.reshape(SPAN_ENTRIES, RECURRENT_GROUPS, P_SIZE)
    gated_out = ssm_out.reshape(SPAN_ENTRIES, RECURRENT_GROUPS * P_SIZE) * jax.nn.silu(gate_input.astype(jnp.float32))
    scaling = lax.rsqrt(lax.optimization_barrier(jnp.mean(gated_out * gated_out, axis=1, keepdims=True)) + eps_norm)
    normed_mix = (gated_out * scaling * norm_gain[None, :]).astype(jnp.bfloat16)
    mixed = jnp.dot(normed_mix, out_proj, preferred_element_type=jnp.float32)
    hidden = residual.astype(jnp.float32) + mixed
    moe_scale = lax.rsqrt(lax.optimization_barrier(jnp.mean(hidden * hidden, axis=1, keepdims=True)) + eps_norm)
    moe_in = (hidden * moe_scale * moe_gain[None, :]).astype(jnp.bfloat16)
    moe_out = experts_apply(moe_in, w_gate, w_up, w_down, route_ids, route_gates)
    return (hidden + moe_out).astype(jnp.bfloat16)
```

```python
import jax
import jax.numpy as jnp
from jax import lax
from jax.sharding import PartitionSpec as P

PAIR = 2
eps_norm = 1e-05
BF = jnp.bfloat16
F32 = jnp.float32
GROUPS = 4


def swap(x, axis, flip):
    size = lax.axis_size(axis)
    return lax.ppermute(x, axis, [(i, i ^ flip) for i in range(size)])


def mm(a, b):
    return jnp.dot(a, b, preferred_element_type=F32)


def split_total(total):
    high = total.astype(BF)
    low = (total - high.astype(F32)).astype(BF)
    both = jnp.concatenate([high, low])
    return jnp.broadcast_to(both[:, None], (both.shape[0], 128))


def with_total(state, total):
    return jnp.concatenate([state.astype(BF), split_total(total)], axis=0)


def apart(packed, heads):
    rows = packed.shape[0] - 2 * heads
    tail = packed[rows:, 0].astype(F32)
    return packed[:rows].astype(F32), tail[:heads] + tail[heads:]


def incoming_state(state, total, start, head_dim):
    place = lax.axis_index("ctx")
    pairs = lax.axis_size("ctx") // 2
    odd = place % 2 == 1
    z = place // 2
    heads = total.shape[0]
    half = heads // 2
    cut = half * head_dim
    keep = jnp.where(odd, state[cut:], state[:cut])
    keep_total = jnp.where(odd, total[half:], total[:half])
    give = jnp.where(odd, state[:cut], state[cut:])
    give_total = jnp.where(odd, total[:half], total[half:])
    got, got_total = apart(swap(with_total(give, give_total), "ctx", 1), half)

    def spread(v):
        return jnp.repeat(v, head_dim)[:, None]

    first = jnp.where(odd, got, keep)
    first_total = jnp.where(odd, got_total, keep_total)
    second = jnp.where(odd, keep, got)
    second_total = jnp.where(odd, keep_total, got_total)
    pair_state = spread(jnp.exp(-second_total)) * first + second
    pair_total = first_total + second_total
    packed = with_total(pair_state, pair_total)
    others = [apart(swap(packed, "ctx", 2 * d), half) for d in range(1, pairs)]
    states = [o[0] for o in others]
    totals = jnp.stack([o[1] for o in others])
    planes = jnp.stack([z ^ d for d in range(1, pairs)])
    between = (planes[None, :] > planes[:, None]) & (planes[None, :] < z)
    gap = jnp.sum(jnp.where(between[:, :, None], totals[None], 0.0), axis=1)
    weight = jnp.where((planes < z)[:, None], jnp.exp(-gap), 0.0)
    before = jnp.sum(jnp.where((planes < z)[:, None], totals, 0.0), axis=0)
    own_start = jnp.where(odd, start[cut:], start[:cut])
    prefix = spread(jnp.exp(-before)) * own_start
    for i, s in enumerate(states):
        prefix = prefix + spread(weight[i]) * s
    later = spread(jnp.exp(-first_total)) * prefix + first
    mine = jnp.where(odd, later, prefix).astype(BF)
    other = swap(jnp.where(odd, prefix, later).astype(BF), "ctx", 1)
    return jnp.where(odd, other, mine), jnp.where(odd, mine, other)


def mixer_rows(inputs, gate_input, b_proj, c_proj, step_size, decay_rate, skip_gain, start_state):
    tok = inputs.shape[0]
    heads = step_size.shape[0]
    width = inputs.shape[1]
    head_dim = width // heads
    cumulative = jnp.cumsum(decay_rate, axis=1)
    total = cumulative[:, -1]

    def wide(v):
        return jnp.broadcast_to(v.T[:, :, None], (tok, heads, head_dim)).reshape(tok, width)

    x_local = inputs.astype(F32)
    ending = jnp.exp(-(total[:, None] - cumulative)) * step_size
    decayed = (x_local * wide(ending)).astype(BF)
    state = lax.dot_general(decayed, b_proj, (((0,), (0,)), ((), ())), preferred_element_type=F32)
    low, high = incoming_state(state, total, start_state.reshape(width, -1), head_dim)
    order = jnp.arange(tok, dtype=jnp.int32)
    causal = order[:, None] >= order[None, :]
    spread = jnp.where(causal[None], cumulative[:, :, None] - cumulative[:, None, :], 0.0)
    scores = lax.dot_general(c_proj, b_proj, (((1,), (1,)), ((), ())), preferred_element_type=F32)
    mixing = jnp.where(causal[None], jnp.exp(-spread), 0.0) * scores[None] * step_size[:, None, :]
    inside = jnp.einsum(
        "hts,shp->thp",
        mixing.astype(BF),
        inputs.reshape(tok, heads, head_dim),
        preferred_element_type=F32,
    ).reshape(tok, width)
    direct = inside + jnp.repeat(skip_gain, head_dim)[None, :] * x_local
    side = (((1,), (1,)), ((), ()))
    carried = jnp.concatenate(
        [
            lax.dot_general(c_proj, low, side, preferred_element_type=F32),
            lax.dot_general(c_proj, high, side, preferred_element_type=F32),
        ],
        axis=1,
    )
    ssm_out = direct + carried * wide(jnp.exp(-cumulative))
    return ssm_out * jax.nn.silu(gate_input.astype(F32))


def project_rows(gated, norm_gain, out_proj):
    n_exp = lax.axis_size("exp")
    n_ctx = lax.axis_size("ctx")
    me_exp = lax.axis_index("exp")
    me_ctx = lax.axis_index("ctx")
    tok, width = gated.shape
    quarter = tok // n_exp
    both = jnp.concatenate([out_proj, swap(out_proj, "ctx", 2)], axis=1)
    squares = jnp.sum(gated * gated, axis=1)
    for flip in (1, 2):
        squares = squares + swap(squares, "exp", flip)
    own_squares = lax.dynamic_slice_in_dim(squares, me_exp * quarter, quarter, 0)
    scale = lax.rsqrt(own_squares / (width * n_exp) + eps_norm)

    rows = (gated * norm_gain[None, :]).astype(BF)
    rel = [0, 2, 1, 3]
    pieces = [lax.dynamic_slice_in_dim(rows, (me_exp ^ q) * quarter, quarter, 0) for q in rel]
    part_a = jnp.concatenate(pieces[:2])
    part_b = jnp.concatenate(pieces[2:])
    hops = [4 * m for m in range(1, n_ctx // 4)]
    a_z = jnp.stack([part_a] + [swap(part_a, "ctx", h) for h in hops])
    b_y = jnp.stack([part_b, swap(part_b, "ctx", 1)])
    a_all = jnp.stack([a_z, swap(a_z, "ctx", 1)])
    b_all = jnp.stack([b_y] + [swap(b_y, "ctx", h) for h in hops])
    a_all = a_all.swapaxes(0, 1)
    group = [h + y for h in [0] + hops for y in (0, 1)]
    full = jnp.concatenate([a_all, b_all], axis=2).reshape(len(group), n_exp, quarter, width)
    full = full.swapaxes(0, 1).reshape(-1, width)
    partial = mm(full, both).astype(BF)
    for flip in (1, 2):
        cut = partial.shape[0] // 2
        got = swap(partial[cut:], "exp", flip)
        partial = (partial[:cut].astype(F32) + got.astype(F32)).astype(BF)
    partial = partial.reshape(len(group), quarter, -1)
    columns = out_proj.shape[1]
    blocks = [None] * n_ctx
    for i, r in enumerate(group):
        block = partial[i] if r == 0 else swap(partial[i], "ctx", r)
        blocks[r] = block[:, :columns]
        blocks[r ^ 2] = block[:, columns:]
    stacked = jnp.stack(blocks)
    place = me_ctx ^ jnp.arange(n_ctx, dtype=jnp.int32)
    mixed = jnp.concatenate(
        [lax.dynamic_index_in_dim(stacked, place[b], 0, False) for b in range(n_ctx)], axis=1
    )
    return mixed.astype(F32), scale


def gather_plane(pieces):
    half = pieces.shape[1] // 2
    width = pieces.shape[2]
    part_a = pieces[:, :half].reshape(-1, width)
    part_b = pieces[:, half:].reshape(-1, width)
    part_a = jnp.concatenate([part_a, swap(part_a, "ctx", 1)])
    part_b = jnp.concatenate([part_b, swap(part_b, "exp", 2)])
    part_a2 = swap(part_a, "exp", 2)
    part_b2 = swap(part_b, "ctx", 1)
    rows = jnp.concatenate([part_a, part_a2, part_b, part_b2])
    return jnp.concatenate([rows, swap(rows, "exp", 1)])


def scatter_plane(rows, count):
    def fold(values, axis, flip):
        cut = values.shape[0] // 2
        got = swap(values[cut:], axis, flip)
        return (values[:cut].astype(F32) + got.astype(F32)).astype(BF)

    rows = fold(rows, "exp", 1)
    cut = rows.shape[0] // 2
    part_a = fold(fold(rows[:cut], "exp", 2), "ctx", 1)
    part_b = fold(fold(rows[cut:], "ctx", 1), "exp", 2)
    width = rows.shape[1]
    part_a = part_a.reshape(count, -1, width)
    part_b = part_b.reshape(count, -1, width)
    return jnp.concatenate([part_a, part_b], axis=1)


def local(
    inputs,
    gate_input,
    b_proj,
    c_proj,
    step_size,
    decay_rate,
    skip_gain,
    start_state,
    norm_gain,
    out_proj,
    residual,
    moe_gain,
    w_gate,
    w_up,
    w_down,
    route_ids,
    route_gates,
):
    n_ctx = lax.axis_size("ctx")
    n_exp = lax.axis_size("exp")
    me_ctx = lax.axis_index("ctx")
    me_exp = lax.axis_index("exp")
    tok = inputs.shape[0]
    quarter = tok // n_exp
    pairs = n_ctx // 2
    experts = n_ctx // PAIR
    named = route_ids[:, :, None] == jnp.arange(experts, dtype=jnp.int32)[None, None, :]
    weights = jnp.sum(jnp.where(named, route_gates[:, :, None], 0.0), axis=1)
    weights_all = lax.all_gather(weights, "ctx")
    own_weight = lax.dynamic_index_in_dim(weights_all, me_ctx // PAIR, 2, False)
    own_weight = own_weight.reshape(n_ctx, n_exp, quarter)

    gated = mixer_rows(
        inputs, gate_input, b_proj, c_proj, step_size, decay_rate, skip_gain, start_state
    )
    mixed, scale = project_rows(gated, norm_gain, out_proj)
    own_residual = lax.dynamic_slice_in_dim(residual, me_exp * quarter, quarter, 0)
    hidden = own_residual.astype(F32) + mixed * scale[:, None]
    moe_scale = lax.rsqrt(jnp.mean(hidden * hidden, axis=1, keepdims=True) + eps_norm)
    moe_in = (hidden * moe_scale * moe_gain[None, :]).astype(BF)

    planes = [moe_in] + [swap(moe_in, "ctx", 2 * d) for d in range(1, pairs)]
    gate_rows, up_rows, down_rows = w_gate[0], w_up[0], w_down[0]
    half = quarter // 2
    order = [(x, y, "a") for x in (0, 1) for y in (0, 1)]
    order = order + [(x, y, "b") for y in (0, 1) for x in (0, 1)]
    total = hidden
    size = pairs // GROUPS
    for first in range(0, pairs, size):
        offsets = list(range(first, first + size))
        rows = gather_plane(jnp.stack([planes[d] for d in offsets]))
        row_weight = []
        for k in (0, 1):
            for x, y, part in order:
                for d in offsets:
                    whole = own_weight[me_ctx ^ (2 * d + y), me_exp ^ (2 * x + k)]
                    row_weight.append(whole[:half] if part == "a" else whole[half:])
        row_weight = jnp.concatenate(row_weight)
        gate_val = mm(rows, gate_rows)
        up_val = mm(rows, up_rows)
        activated = (jax.nn.silu(gate_val) * up_val).astype(BF)
        result = (mm(activated, down_rows) * row_weight[:, None]).astype(BF)
        summed = scatter_plane(result, size)
        for i, d in enumerate(offsets):
            back = summed[i] if d == 0 else swap(summed[i], "ctx", 2 * d)
            total = total + back.astype(F32)
    return total.astype(BF)


def solution(mesh):
    in_specs = (
        P("ctx", "exp"),
        P("ctx", "exp"),
        P("ctx", None),
        P("ctx", None),
        P("exp", "ctx"),
        P("exp", "ctx"),
        P("exp"),
        P("exp", None, None),
        P("exp"),
        P("exp", "ctx"),
        P("ctx", None),
        P(),
        P("ctx", None, "exp"),
        P("ctx", None, "exp"),
        P("ctx", "exp", None),
        P("ctx", None),
        P("ctx", None),
    )
    out_specs = P(("ctx", "exp"), None)
    return jax.shard_map(local, mesh=mesh, in_specs=in_specs, out_specs=out_specs, check_vma=False)
```

```python
import jax
import jax.numpy as jnp
from jax import lax
from jax.experimental import pallas as pl
from jax.experimental.pallas import tpu as pltpu
from jax.sharding import PartitionSpec as P

PAIR = 2
eps_norm = 1e-05
BF = jnp.bfloat16
F32 = jnp.float32
LANES = 128
DOWN_TILE = 512


def swap(x, axis, flip):
    size = lax.axis_size(axis)
    return lax.ppermute(x, axis, [(i, i ^ flip) for i in range(size)])


def mm(a, b):
    return jnp.dot(a, b, preferred_element_type=F32)


def split_total(total):
    high = total.astype(BF)
    low = (total - high.astype(F32)).astype(BF)
    both = jnp.concatenate([high, low])
    return jnp.broadcast_to(both[:, None], (both.shape[0], 128))


def with_total(state, total):
    return jnp.concatenate([state.astype(BF), split_total(total)], axis=0)


def apart(packed, heads):
    rows = packed.shape[0] - 2 * heads
    tail = packed[rows:, 0].astype(F32)
    return packed[:rows].astype(F32), tail[:heads] + tail[heads:]


def incoming_state(state, total, start, head_dim):
    place = lax.axis_index("ctx")
    pairs = lax.axis_size("ctx") // 2
    odd = place % 2 == 1
    z = place // 2
    heads = total.shape[0]
    half = heads // 2
    cut = half * head_dim
    keep = jnp.where(odd, state[cut:], state[:cut])
    keep_total = jnp.where(odd, total[half:], total[:half])
    give = jnp.where(odd, state[:cut], state[cut:])
    give_total = jnp.where(odd, total[:half], total[half:])
    got, got_total = apart(swap(with_total(give, give_total), "ctx", 1), half)

    def spread(v):
        return jnp.repeat(v, head_dim)[:, None]

    first = jnp.where(odd, got, keep)
    first_total = jnp.where(odd, got_total, keep_total)
    second = jnp.where(odd, keep, got)
    second_total = jnp.where(odd, keep_total, got_total)
    pair_state = spread(jnp.exp(-second_total)) * first + second
    pair_total = first_total + second_total
    packed = with_total(pair_state, pair_total)
    others = [apart(swap(packed, "ctx", 2 * d), half) for d in range(1, pairs)]
    states = [o[0] for o in others]
    totals = jnp.stack([o[1] for o in others])
    planes = jnp.stack([z ^ d for d in range(1, pairs)])
    between = (planes[None, :] > planes[:, None]) & (planes[None, :] < z)
    gap = jnp.sum(jnp.where(between[:, :, None], totals[None], 0.0), axis=1)
    weight = jnp.where((planes < z)[:, None], jnp.exp(-gap), 0.0)
    before = jnp.sum(jnp.where((planes < z)[:, None], totals, 0.0), axis=0)
    own_start = jnp.where(odd, start[cut:], start[:cut])
    prefix = spread(jnp.exp(-before)) * own_start
    for i, s in enumerate(states):
        prefix = prefix + spread(weight[i]) * s
    later = spread(jnp.exp(-first_total)) * prefix + first
    mine = jnp.where(odd, later, prefix).astype(BF)
    other = swap(jnp.where(odd, prefix, later).astype(BF), "ctx", 1)
    return jnp.where(odd, other, mine), jnp.where(odd, mine, other)


def mixer_rows(inputs, gate_input, b_proj, c_proj, step_size, decay_rate, skip_gain, start_state):
    tok = inputs.shape[0]
    heads = step_size.shape[0]
    width = inputs.shape[1]
    head_dim = width // heads
    cumulative = jnp.cumsum(decay_rate, axis=1)
    total = cumulative[:, -1]

    def wide(v):
        return jnp.broadcast_to(v.T[:, :, None], (tok, heads, head_dim)).reshape(tok, width)

    x_local = inputs.astype(F32)
    ending = jnp.exp(-(total[:, None] - cumulative)) * step_size
    decayed = (x_local * wide(ending)).astype(BF)
    state = lax.dot_general(decayed, b_proj, (((0,), (0,)), ((), ())), preferred_element_type=F32)
    low, high = incoming_state(state, total, start_state.reshape(width, -1), head_dim)
    order = jnp.arange(tok, dtype=jnp.int32)
    causal = order[:, None] >= order[None, :]
    spread = jnp.where(causal[None], cumulative[:, :, None] - cumulative[:, None, :], 0.0)
    scores = lax.dot_general(c_proj, b_proj, (((1,), (1,)), ((), ())), preferred_element_type=F32)
    mixing = jnp.where(causal[None], jnp.exp(-spread), 0.0) * scores[None] * step_size[:, None, :]
    inside = jnp.einsum(
        "hts,shp->thp",
        mixing.astype(BF),
        inputs.reshape(tok, heads, head_dim),
        preferred_element_type=F32,
    ).reshape(tok, width)
    direct = inside + jnp.repeat(skip_gain, head_dim)[None, :] * x_local
    side = (((1,), (1,)), ((), ()))
    carried = jnp.concatenate(
        [
            lax.dot_general(c_proj, low, side, preferred_element_type=F32),
            lax.dot_general(c_proj, high, side, preferred_element_type=F32),
        ],
        axis=1,
    )
    ssm_out = direct + carried * wide(jnp.exp(-cumulative))
    return ssm_out * jax.nn.silu(gate_input.astype(F32))


def project_rows(gated, norm_gain, out_proj):
    n_exp = lax.axis_size("exp")
    n_ctx = lax.axis_size("ctx")
    me_exp = lax.axis_index("exp")
    me_ctx = lax.axis_index("ctx")
    tok, width = gated.shape
    quarter = tok // n_exp
    both = jnp.concatenate([out_proj, swap(out_proj, "ctx", 2)], axis=1)
    squares = jnp.sum(gated * gated, axis=1)
    for flip in (1, 2):
        squares = squares + swap(squares, "exp", flip)
    own_squares = lax.dynamic_slice_in_dim(squares, me_exp * quarter, quarter, 0)
    scale = lax.rsqrt(own_squares / (width * n_exp) + eps_norm)

    rows = (gated * norm_gain[None, :]).astype(BF)
    rel = [0, 2, 1, 3]
    pieces = [lax.dynamic_slice_in_dim(rows, (me_exp ^ q) * quarter, quarter, 0) for q in rel]
    part_a = jnp.concatenate(pieces[:2])
    part_b = jnp.concatenate(pieces[2:])
    hops = [4 * m for m in range(1, n_ctx // 4)]
    a_z = jnp.stack([part_a] + [swap(part_a, "ctx", h) for h in hops])
    b_y = jnp.stack([part_b, swap(part_b, "ctx", 1)])
    a_all = jnp.stack([a_z, swap(a_z, "ctx", 1)])
    b_all = jnp.stack([b_y] + [swap(b_y, "ctx", h) for h in hops])
    a_all = a_all.swapaxes(0, 1)
    group = [h + y for h in [0] + hops for y in (0, 1)]
    full = jnp.concatenate([a_all, b_all], axis=2).reshape(len(group), n_exp, quarter, width)
    full = full.swapaxes(0, 1).reshape(-1, width)
    partial = mm(full, both).astype(BF)
    for flip in (1, 2):
        cut = partial.shape[0] // 2
        got = swap(partial[cut:], "exp", flip)
        partial = (partial[:cut].astype(F32) + got.astype(F32)).astype(BF)
    partial = partial.reshape(len(group), quarter, -1)
    columns = out_proj.shape[1]
    blocks = [None] * n_ctx
    for i, r in enumerate(group):
        block = partial[i] if r == 0 else swap(partial[i], "ctx", r)
        blocks[r] = block[:, :columns]
        blocks[r ^ 2] = block[:, columns:]
    stacked = jnp.stack(blocks)
    place = me_ctx ^ jnp.arange(n_ctx, dtype=jnp.int32)
    mixed = jnp.concatenate(
        [lax.dynamic_index_in_dim(stacked, place[b], 0, False) for b in range(n_ctx)], axis=1
    )
    return mixed.astype(F32), scale


def pack_kernel(*refs):
    pieces, out, sems = refs[:-2], refs[-2], refs[-1]
    copies = []
    row = 0
    for i, piece in enumerate(pieces):
        rows = piece.shape[0]
        copies.append(pltpu.make_async_copy(piece, out.at[pl.ds(row, rows)], sems.at[i]))
        row += rows
    for c in copies:
        c.start()
    for c in copies:
        c.wait()


def pack(pieces):
    rows = sum(p.shape[0] for p in pieces)
    width = pieces[0].shape[1]
    size = 2 * rows * width
    return pl.pallas_call(
        pack_kernel,
        out_shape=jax.ShapeDtypeStruct((rows, width), pieces[0].dtype),
        in_specs=[pl.BlockSpec(memory_space=pl.ANY)] * len(pieces),
        out_specs=pl.BlockSpec(memory_space=pl.ANY),
        scratch_shapes=[pltpu.SemaphoreType.DMA((len(pieces),))],
        cost_estimate=pl.CostEstimate(flops=0, bytes_accessed=2 * size, transcendentals=0),
    )(*pieces)


def expert_kernel(
    own, mate, gate, up, down, pick, out_own, out_mate, rows, hidden, gu, dn, row_sem, gu_sem, dn_sem
):
    half = own.shape[0]
    model = gate.shape[0]
    tiles = gate.shape[1] // LANES
    down_tiles = model // DOWN_TILE

    def row_copies():
        return [
            pltpu.make_async_copy(own, rows.at[pl.ds(0, half)], row_sem.at[0]),
            pltpu.make_async_copy(mate, rows.at[pl.ds(half, half)], row_sem.at[1]),
        ]

    def gu_copies(j, slot):
        at = pl.ds(pl.multiple_of(j * LANES, LANES), LANES)
        return [
            pltpu.make_async_copy(gate.at[:, at], gu.at[slot, :, pl.ds(0, LANES)], gu_sem.at[slot, 0]),
            pltpu.make_async_copy(up.at[:, at], gu.at[slot, :, pl.ds(LANES, LANES)], gu_sem.at[slot, 1]),
        ]

    def dn_copy(j, slot):
        at = pl.ds(pl.multiple_of(j * DOWN_TILE, DOWN_TILE), DOWN_TILE)
        return pltpu.make_async_copy(down.at[:, at], dn.at[slot], dn_sem.at[slot])

    for c in row_copies() + gu_copies(0, 0):
        c.start()
    dn_copy(0, 0).start()
    for c in row_copies():
        c.wait()

    def gate_up(j, carry):
        slot = lax.rem(j, 2)

        @pl.when(j + 1 < tiles)
        def _():
            for c in gu_copies(j + 1, lax.rem(j + 1, 2)):
                c.start()

        for c in gu_copies(j, slot):
            c.wait()
        both = jnp.dot(rows[:, :model], gu[slot], preferred_element_type=F32)
        gate_val = both[:, :LANES]
        act = gate_val / (1.0 + jnp.exp(-gate_val)) * both[:, LANES:]
        hidden[:, pl.ds(pl.multiple_of(j * LANES, LANES), LANES)] = act.astype(BF)
        return carry

    lax.fori_loop(0, tiles, gate_up, 0)
    weight = jnp.sum(rows[:, model:].astype(F32) * pick[...], axis=1, keepdims=True)

    def down_part(j, carry):
        slot = lax.rem(j, 2)

        @pl.when(j + 1 < down_tiles)
        def _():
            dn_copy(j + 1, lax.rem(j + 1, 2)).start()

        dn_copy(j, slot).wait()
        part = jnp.dot(hidden[...], dn[slot], preferred_element_type=F32) * weight
        at = pl.ds(pl.multiple_of(j * DOWN_TILE, DOWN_TILE), DOWN_TILE)
        out_own[:, at] = part[:half].astype(BF)
        out_mate[:, at] = part[half:].astype(BF)
        return carry

    lax.fori_loop(0, down_tiles, down_part, 0)


def experts(own, mate, gate, up, down, pick):
    half, width = own.shape
    model, units = gate.shape
    out = jax.ShapeDtypeStruct((half, model), BF)
    whole = pl.BlockSpec(memory_space=pltpu.VMEM)
    anywhere = pl.BlockSpec(memory_space=pl.ANY)
    flops = 2 * 2 * half * model * units * 3
    moved = 2 * (3 * model * units + 8 * half * model)
    return pl.pallas_call(
        expert_kernel,
        out_shape=(out, out),
        in_specs=[anywhere] * 5 + [whole],
        out_specs=(whole, whole),
        scratch_shapes=[
            pltpu.VMEM((2 * half, width), BF),
            pltpu.VMEM((2 * half, units), BF),
            pltpu.VMEM((2, model, 2 * LANES), BF),
            pltpu.VMEM((2, units, DOWN_TILE), BF),
            pltpu.SemaphoreType.DMA((2,)),
            pltpu.SemaphoreType.DMA((2, 2)),
            pltpu.SemaphoreType.DMA((2,)),
        ],
        compiler_params=pltpu.CompilerParams(vmem_limit_bytes=40 * 1024 * 1024),
        cost_estimate=pl.CostEstimate(flops=flops, bytes_accessed=moved, transcendentals=2 * half * units),
    )(own, mate, gate, up, down, pick)


def gather_plane(piece):
    half = piece.shape[0] // 2
    from_x = swap(piece, "exp", 2)
    from_y = swap(piece, "ctx", 1)
    far_a = swap(from_y[:half], "exp", 2)
    far_b = swap(from_x[half:], "ctx", 1)
    return pack([piece, from_x, from_y, far_a, far_b])


def scatter_plane(own, mate):
    got = swap(mate, "exp", 1)
    size = own.shape[0] // 4
    half = size // 2

    def both(first, rows):
        last = first + rows
        return own[first:last].astype(F32) + got[first:last].astype(F32)

    far_a = swap(both(3 * size, half).astype(BF), "exp", 2)
    far_b = swap(both(3 * size + half, half).astype(BF), "ctx", 1)
    to_x = both(size, size)
    to_y = both(2 * size, size)
    to_y = jnp.concatenate([to_y[:half] + far_a.astype(F32), to_y[half:]])
    to_x = jnp.concatenate([to_x[:half], to_x[half:] + far_b.astype(F32)])
    from_x = swap(to_x.astype(BF), "exp", 2)
    from_y = swap(to_y.astype(BF), "ctx", 1)
    return both(0, size) + from_x.astype(F32) + from_y.astype(F32)


def local(
    inputs,
    gate_input,
    b_proj,
    c_proj,
    step_size,
    decay_rate,
    skip_gain,
    start_state,
    norm_gain,
    out_proj,
    residual,
    moe_gain,
    w_gate,
    w_up,
    w_down,
    route_ids,
    route_gates,
):
    n_ctx = lax.axis_size("ctx")
    n_exp = lax.axis_size("exp")
    me_ctx = lax.axis_index("ctx")
    me_exp = lax.axis_index("exp")
    tok = inputs.shape[0]
    quarter = tok // n_exp
    pairs = n_ctx // 2
    named = route_ids[:, :, None] == jnp.arange(LANES // 2, dtype=jnp.int32)[None, None, :]
    weights = jnp.sum(jnp.where(named, route_gates[:, :, None], 0.0), axis=1)
    weights = lax.dynamic_slice_in_dim(weights, me_exp * quarter, quarter, 0)
    weights_high = weights.astype(BF)
    weights_low = (weights - weights_high.astype(F32)).astype(BF)
    lane = jnp.arange(LANES, dtype=jnp.int32)
    pick = (lane % (LANES // 2) == me_ctx // PAIR).astype(F32)[None, :]

    gated = mixer_rows(
        inputs, gate_input, b_proj, c_proj, step_size, decay_rate, skip_gain, start_state
    )
    mixed, scale = project_rows(gated, norm_gain, out_proj)
    own_residual = lax.dynamic_slice_in_dim(residual, me_exp * quarter, quarter, 0)
    hidden = own_residual.astype(F32) + mixed * scale[:, None]
    moe_scale = lax.rsqrt(jnp.mean(hidden * hidden, axis=1, keepdims=True) + eps_norm)
    moe_in = (hidden * moe_scale * moe_gain[None, :]).astype(BF)

    payload = jnp.concatenate([moe_in, weights_high, weights_low], axis=1)
    planes = [payload] + [swap(payload, "ctx", 2 * d) for d in range(1, pairs)]
    total = hidden
    groups = [[0], [1]] + [[d, d + 1] for d in range(2, pairs, 2)]
    for offsets in groups:
        piece = planes[offsets[0]] if len(offsets) == 1 else pack([planes[d] for d in offsets])
        own = gather_plane(piece)
        mate = swap(own, "exp", 1)
        own, mate = experts(own, mate, w_gate[0], w_up[0], w_down[0], pick)
        summed = scatter_plane(own, mate)
        for i, d in enumerate(offsets):
            part = summed[i * quarter : (i + 1) * quarter]
            total = total + (part if d == 0 else swap(part.astype(BF), "ctx", 2 * d).astype(F32))
    return total.astype(BF)


def solution(mesh):
    in_specs = (
        P("ctx", "exp"),
        P("ctx", "exp"),
        P("ctx", None),
        P("ctx", None),
        P("exp", "ctx"),
        P("exp", "ctx"),
        P("exp"),
        P("exp", None, None),
        P("exp"),
        P("exp", "ctx"),
        P("ctx", None),
        P(),
        P("ctx", None, "exp"),
        P("ctx", None, "exp"),
        P("ctx", "exp", None),
        P("ctx", None),
        P("ctx", None),
    )
    out_specs = P(("ctx", "exp"), None)
    return jax.shard_map(local, mesh=mesh, in_specs=in_specs, out_specs=out_specs, check_vma=False)
```

```python
import jax
import jax.numpy as jnp
from jax import lax
from jax.experimental import pallas as pl
from jax.experimental.pallas import tpu as pltpu
from jax.sharding import PartitionSpec as P

PAIR = 2
eps_norm = 1e-05
BF = jnp.bfloat16
F32 = jnp.float32
LANES = 128
DOWN_TILE = 1024
GU_SLOTS = 4
DN_SLOTS = 3


def swap(x, axis, flip):
    size = lax.axis_size(axis)
    return lax.ppermute(x, axis, [(i, i ^ flip) for i in range(size)])


def mm(a, b):
    return jnp.dot(a, b, preferred_element_type=F32)


def split_total(total):
    high = total.astype(BF)
    low = (total - high.astype(F32)).astype(BF)
    both = jnp.concatenate([high, low])
    return jnp.broadcast_to(both[:, None], (both.shape[0], 128))


def with_total(state, total):
    return jnp.concatenate([state.astype(BF), split_total(total)], axis=0)


def apart(packed, heads):
    rows = packed.shape[0] - 2 * heads
    tail = packed[rows:, 0].astype(F32)
    return packed[:rows].astype(F32), tail[:heads] + tail[heads:]


def incoming_state(state, total, start, head_dim, later_use):
    place = lax.axis_index("ctx")
    pairs = lax.axis_size("ctx") // 2
    odd = place % 2 == 1
    z = place // 2
    heads = total.shape[0]
    half = heads // 2
    cut = half * head_dim
    keep = jnp.where(odd, state[cut:], state[:cut])
    keep_total = jnp.where(odd, total[half:], total[:half])
    give = jnp.where(odd, state[:cut], state[cut:])
    give_total = jnp.where(odd, total[:half], total[half:])
    got, got_total = apart(swap(with_total(give, give_total), "ctx", 1), half)

    def spread(v):
        return jnp.repeat(v, head_dim)[:, None]

    first = jnp.where(odd, got, keep)
    first_total = jnp.where(odd, got_total, keep_total)
    second = jnp.where(odd, keep, got)
    second_total = jnp.where(odd, keep_total, got_total)
    pair_state = spread(jnp.exp(-second_total)) * first + second
    pair_total = first_total + second_total
    packed = with_total(pair_state, pair_total)
    others = [apart(swap(packed, "ctx", 2 * d), half) for d in range(1, pairs)]
    states = [o[0] for o in others]
    totals = jnp.stack([o[1] for o in others])
    planes = jnp.stack([z ^ d for d in range(1, pairs)])
    between = (planes[None, :] > planes[:, None]) & (planes[None, :] < z)
    gap = jnp.sum(jnp.where(between[:, :, None], totals[None], 0.0), axis=1)
    weight = jnp.where((planes < z)[:, None], jnp.exp(-gap), 0.0)
    before = jnp.sum(jnp.where((planes < z)[:, None], totals, 0.0), axis=0)
    states, later_use = lax.optimization_barrier((states, later_use))
    own_start = jnp.where(odd, start[cut:], start[:cut])
    prefix = spread(jnp.exp(-before)) * own_start
    for i, s in enumerate(states):
        prefix = prefix + spread(weight[i]) * s
    later = spread(jnp.exp(-first_total)) * prefix + first
    mine = jnp.where(odd, later, prefix).astype(BF)
    other = swap(jnp.where(odd, prefix, later).astype(BF), "ctx", 1)
    return jnp.where(odd, other, mine), jnp.where(odd, mine, other), later_use


def mixer_rows(
    inputs, gate_input, b_proj, c_proj, step_size, decay_rate, skip_gain, start_state, later_use
):
    tok = inputs.shape[0]
    heads = step_size.shape[0]
    width = inputs.shape[1]
    head_dim = width // heads
    cumulative = jnp.cumsum(decay_rate, axis=1)
    total = cumulative[:, -1]

    def wide(v):
        return jnp.broadcast_to(v.T[:, :, None], (tok, heads, head_dim)).reshape(tok, width)

    x_local = inputs.astype(F32)
    ending = jnp.exp(-(total[:, None] - cumulative)) * step_size
    decayed = (x_local * wide(ending)).astype(BF)
    state = lax.dot_general(decayed, b_proj, (((0,), (0,)), ((), ())), preferred_element_type=F32)
    low, high, later_use = incoming_state(
        state, total, start_state.reshape(width, -1), head_dim, later_use
    )
    order = jnp.arange(tok, dtype=jnp.int32)
    causal = order[:, None] >= order[None, :]
    spread = jnp.where(causal[None], cumulative[:, :, None] - cumulative[:, None, :], 0.0)
    scores = lax.dot_general(c_proj, b_proj, (((1,), (1,)), ((), ())), preferred_element_type=F32)
    mixing = jnp.where(causal[None], jnp.exp(-spread), 0.0) * scores[None] * step_size[:, None, :]
    inside = jnp.einsum(
        "hts,shp->thp",
        mixing.astype(BF),
        inputs.reshape(tok, heads, head_dim),
        preferred_element_type=F32,
    ).reshape(tok, width)
    direct = inside + jnp.repeat(skip_gain, head_dim)[None, :] * x_local
    side = (((1,), (1,)), ((), ()))
    carried = jnp.concatenate(
        [
            lax.dot_general(c_proj, low, side, preferred_element_type=F32),
            lax.dot_general(c_proj, high, side, preferred_element_type=F32),
        ],
        axis=1,
    )
    ssm_out = direct + carried * wide(jnp.exp(-cumulative))
    return ssm_out * jax.nn.silu(gate_input.astype(F32)), later_use


def project_rows(gated, norm_gain, out_proj, neighbour_proj):
    n_exp = lax.axis_size("exp")
    n_ctx = lax.axis_size("ctx")
    me_exp = lax.axis_index("exp")
    me_ctx = lax.axis_index("ctx")
    tok, width = gated.shape
    quarter = tok // n_exp
    both = jnp.concatenate([out_proj, neighbour_proj], axis=1)
    squares = jnp.sum(gated * gated, axis=1)
    for flip in (1, 2):
        squares = squares + swap(squares, "exp", flip)
    own_squares = lax.dynamic_slice_in_dim(squares, me_exp * quarter, quarter, 0)
    scale = lax.rsqrt(own_squares / (width * n_exp) + eps_norm)

    rows = (gated * norm_gain[None, :]).astype(BF)
    rel = [0, 2, 1, 3]
    pieces = [lax.dynamic_slice_in_dim(rows, (me_exp ^ q) * quarter, quarter, 0) for q in rel]
    part_a = jnp.concatenate(pieces[:2])
    part_b = jnp.concatenate(pieces[2:])
    hops = [4 * m for m in range(1, n_ctx // 4)]
    a_z = jnp.stack([part_a] + [swap(part_a, "ctx", h) for h in hops])
    b_y = jnp.stack([part_b, swap(part_b, "ctx", 1)])
    a_all = jnp.stack([a_z, swap(a_z, "ctx", 1)])
    b_all = jnp.stack([b_y] + [swap(b_y, "ctx", h) for h in hops])
    a_all = a_all.swapaxes(0, 1)
    group = [h + y for h in [0] + hops for y in (0, 1)]
    full = jnp.concatenate([a_all, b_all], axis=2).reshape(len(group), n_exp, quarter, width)
    full = full.swapaxes(0, 1).reshape(-1, width)
    full, scale = lax.optimization_barrier((full, scale))
    partial = mm(full, both).astype(BF)
    for flip in (1, 2):
        cut = partial.shape[0] // 2
        got = swap(partial[cut:], "exp", flip)
        partial = (partial[:cut].astype(F32) + got.astype(F32)).astype(BF)
    partial = partial.reshape(len(group), quarter, -1)
    columns = out_proj.shape[1]
    blocks = [None] * n_ctx
    for i, r in enumerate(group):
        block = partial[i] if r == 0 else swap(partial[i], "ctx", r)
        blocks[r] = block[:, :columns]
        blocks[r ^ 2] = block[:, columns:]
    stacked = jnp.stack(blocks)
    mixed = jnp.concatenate(
        [lax.dynamic_index_in_dim(stacked, me_ctx ^ b, 0, False) for b in range(n_ctx)], axis=1
    )
    return mixed.astype(F32), scale


def pack_kernel(*refs):
    out = refs[-1]
    row = 0
    for piece in refs[:-1]:
        rows = piece.shape[0]
        out[row : row + rows, :] = piece[...]
        row += rows


def pack(pieces):
    rows = sum(p.shape[0] for p in pieces)
    width = pieces[0].shape[1]
    whole = pl.BlockSpec(memory_space=pltpu.VMEM)
    return pl.pallas_call(
        pack_kernel,
        out_shape=jax.ShapeDtypeStruct((rows, width), pieces[0].dtype),
        in_specs=[whole] * len(pieces),
        out_specs=whole,
        compiler_params=pltpu.CompilerParams(vmem_limit_bytes=32 * 1024 * 1024),
        cost_estimate=pl.CostEstimate(flops=0, bytes_accessed=4 * rows * width, transcendentals=0),
    )(*pieces)


def expert_kernel(
    own, mate, gate, up, down, pick, out_own, out_mate, rows, hidden, gu, dn, row_sem, gu_sem, dn_sem
):
    half = own.shape[0]
    model = gate.shape[0]
    tiles = gate.shape[1] // LANES
    down_tiles = model // DOWN_TILE
    row_copies = [
        pltpu.make_async_copy(own, rows.at[pl.ds(0, half)], row_sem.at[0]),
        pltpu.make_async_copy(mate, rows.at[pl.ds(half, half)], row_sem.at[1]),
    ]

    def gu_copies(j):
        at = pl.ds(pl.multiple_of(j * LANES, LANES), LANES)
        s = lax.rem(j, GU_SLOTS)
        return [
            pltpu.make_async_copy(gate.at[:, at], gu.at[s, :, pl.ds(0, LANES)], gu_sem.at[s, 0]),
            pltpu.make_async_copy(up.at[:, at], gu.at[s, :, pl.ds(LANES, LANES)], gu_sem.at[s, 1]),
        ]

    def dn_copy(j):
        at = pl.ds(pl.multiple_of(j * DOWN_TILE, DOWN_TILE), DOWN_TILE)
        s = lax.rem(j, DN_SLOTS)
        return pltpu.make_async_copy(down.at[:, at], dn.at[s], dn_sem.at[s])

    for c in row_copies:
        c.start()
    for j in range(GU_SLOTS - 1):
        for c in gu_copies(j):
            c.start()
    for c in row_copies:
        c.wait()

    def gate_up(j, carry):
        ahead = j + GU_SLOTS - 1
        for c in gu_copies(j):
            c.wait()

        @pl.when(ahead < tiles)
        def _():
            for c in gu_copies(ahead):
                c.start()

        @pl.when((ahead >= tiles) & (ahead - tiles < DN_SLOTS - 1))
        def _():
            dn_copy(ahead - tiles).start()

        both = mm(rows[:, :model], gu[lax.rem(j, GU_SLOTS)])
        gate_val = both[:, :LANES]
        act = gate_val / (1.0 + jnp.exp(-gate_val)) * both[:, LANES:]
        hidden[:, pl.ds(pl.multiple_of(j * LANES, LANES), LANES)] = act.astype(BF)
        return carry

    lax.fori_loop(0, tiles, gate_up, 0)
    weight = jnp.sum(rows[:, model:].astype(F32) * pick[...], axis=1, keepdims=True)

    def down_part(j, carry):
        dn_copy(j).wait()

        @pl.when(j + DN_SLOTS - 1 < down_tiles)
        def _():
            dn_copy(j + DN_SLOTS - 1).start()

        part = mm(hidden[...], dn[lax.rem(j, DN_SLOTS)]) * weight
        at = pl.ds(pl.multiple_of(j * DOWN_TILE, DOWN_TILE), DOWN_TILE)
        out_own[:, at] = part[:half].astype(BF)
        out_mate[:, at] = part[half:].astype(BF)
        return carry

    lax.fori_loop(0, down_tiles, down_part, 0)


def experts(own, mate, gate, up, down, pick):
    half, width = own.shape
    model, units = gate.shape
    out = jax.ShapeDtypeStruct((half, model), BF)
    whole = pl.BlockSpec(memory_space=pltpu.VMEM)
    anywhere = pl.BlockSpec(memory_space=pl.ANY)
    hbm = pl.BlockSpec(memory_space=pltpu.HBM)
    flops = 2 * 2 * half * model * units * 3
    moved = 2 * (3 * model * units + 8 * half * model)
    return pl.pallas_call(
        expert_kernel,
        out_shape=(out, out),
        in_specs=[anywhere] * 2 + [hbm] * 3 + [whole],
        out_specs=(whole, whole),
        scratch_shapes=[
            pltpu.VMEM((2 * half, width), BF),
            pltpu.VMEM((2 * half, units), BF),
            pltpu.VMEM((GU_SLOTS, model, 2 * LANES), BF),
            pltpu.VMEM((DN_SLOTS, units, DOWN_TILE), BF),
            pltpu.SemaphoreType.DMA((2,)),
            pltpu.SemaphoreType.DMA((GU_SLOTS, 2)),
            pltpu.SemaphoreType.DMA((DN_SLOTS,)),
        ],
        compiler_params=pltpu.CompilerParams(vmem_limit_bytes=48 * 1024 * 1024),
        cost_estimate=pl.CostEstimate(flops=flops, bytes_accessed=moved, transcendentals=2 * half * units),
    )(own, mate, gate, up, down, pick)


def gather_plane(piece):
    half = piece.shape[0] // 2
    from_x = swap(piece, "exp", 2)
    from_y = swap(piece, "ctx", 1)
    far_a = swap(from_y[:half], "exp", 2)
    far_b = swap(from_x[half:], "ctx", 1)
    return pack([piece, from_x, from_y, far_a, far_b])


def scatter_plane(own, mate):
    got = swap(mate, "exp", 1)
    size = own.shape[0] // 4
    half = size // 2

    def both(first, rows):
        last = first + rows
        return own[first:last].astype(F32) + got[first:last].astype(F32)

    far_a = swap(both(3 * size, half).astype(BF), "exp", 2)
    far_b = swap(both(3 * size + half, half).astype(BF), "ctx", 1)
    to_x = both(size, size)
    to_y = both(2 * size, size)
    to_y = jnp.concatenate([to_y[:half] + far_a.astype(F32), to_y[half:]])
    to_x = jnp.concatenate([to_x[:half], to_x[half:] + far_b.astype(F32)])
    from_x = swap(to_x.astype(BF), "exp", 2)
    from_y = swap(to_y.astype(BF), "ctx", 1)
    return both(0, size) + from_x.astype(F32) + from_y.astype(F32)


def local(
    inputs,
    gate_input,
    b_proj,
    c_proj,
    step_size,
    decay_rate,
    skip_gain,
    start_state,
    norm_gain,
    out_proj,
    residual,
    moe_gain,
    w_gate,
    w_up,
    w_down,
    route_ids,
    route_gates,
):
    n_ctx = lax.axis_size("ctx")
    n_exp = lax.axis_size("exp")
    me_ctx = lax.axis_index("ctx")
    me_exp = lax.axis_index("exp")
    tok = inputs.shape[0]
    quarter = tok // n_exp
    pairs = n_ctx // 2
    named = route_ids[:, :, None] == jnp.arange(LANES // 2, dtype=jnp.int32)[None, None, :]
    weights = jnp.sum(jnp.where(named, route_gates[:, :, None], 0.0), axis=1)
    weights = lax.dynamic_slice_in_dim(weights, me_exp * quarter, quarter, 0)
    weights_high = weights.astype(BF)
    weights_low = (weights - weights_high.astype(F32)).astype(BF)
    lane = jnp.arange(LANES, dtype=jnp.int32)
    pick = (lane % (LANES // 2) == me_ctx // PAIR).astype(F32)[None, :]

    cut = out_proj.shape[0] // 2
    first_part = swap(out_proj[:cut], "ctx", 2)
    gated, second_part = mixer_rows(
        inputs, gate_input, b_proj, c_proj, step_size, decay_rate, skip_gain, start_state, out_proj[cut:]
    )
    neighbour_proj = jnp.concatenate([first_part, swap(second_part, "ctx", 2)])
    mixed, scale = project_rows(gated, norm_gain, out_proj, neighbour_proj)
    own_residual = lax.dynamic_slice_in_dim(residual, me_exp * quarter, quarter, 0)
    hidden = own_residual.astype(F32) + mixed * scale[:, None]
    moe_scale = lax.rsqrt(jnp.mean(hidden * hidden, axis=1, keepdims=True) + eps_norm)
    moe_in = (hidden * moe_scale * moe_gain[None, :]).astype(BF)

    payload = jnp.concatenate([moe_in, weights_high, weights_low], axis=1)
    planes = [payload] + [swap(payload, "ctx", 2 * d) for d in range(1, pairs)]
    total = hidden
    groups = [[0], [1]] + [[d, d + 1] for d in range(2, pairs, 2)]
    for offsets in groups:
        piece = planes[offsets[0]] if len(offsets) == 1 else pack([planes[d] for d in offsets])
        own = gather_plane(piece)
        mate = swap(own, "exp", 1)
        own, mate = experts(own, mate, w_gate[0], w_up[0], w_down[0], pick)
        summed = scatter_plane(own, mate)
        for i, d in enumerate(offsets):
            part = summed[i * quarter : (i + 1) * quarter]
            total = total + (part if d == 0 else swap(part.astype(BF), "ctx", 2 * d).astype(F32))
    return total.astype(BF)


def solution(mesh):
    in_specs = (
        P("ctx", "exp"),
        P("ctx", "exp"),
        P("ctx", None),
        P("ctx", None),
        P("exp", "ctx"),
        P("exp", "ctx"),
        P("exp"),
        P("exp", None, None),
        P("exp"),
        P("exp", "ctx"),
        P("ctx", None),
        P(),
        P("ctx", None, "exp"),
        P("ctx", None, "exp"),
        P("ctx", "exp", None),
        P("ctx", None),
        P("ctx", None),
    )
    out_specs = P(("ctx", "exp"), None)
    return jax.shard_map(local, mesh=mesh, in_specs=in_specs, out_specs=out_specs, check_vma=False)
```

```python
import jax
import jax.numpy as jnp
from jax import lax
from jax.experimental import pallas as pl
from jax.experimental.pallas import tpu as pltpu
from jax.sharding import PartitionSpec as P

PAIR = 2
eps_norm = 1e-05
BF = jnp.bfloat16
F32 = jnp.float32
LANES = 128
DOWN_TILE = 1024
GU_SLOTS = 4
DN_SLOTS = 3


def swap(x, axis, flip):
    size = lax.axis_size(axis)
    return lax.ppermute(x, axis, [(i, i ^ flip) for i in range(size)])


def mm(a, b):
    return jnp.dot(a, b, preferred_element_type=F32)


def split_total(total):
    high = total.astype(BF)
    low = (total - high.astype(F32)).astype(BF)
    both = jnp.concatenate([high, low])
    return jnp.broadcast_to(both[:, None], (both.shape[0], 128))


def with_total(state, total):
    return jnp.concatenate([state.astype(BF), split_total(total)], axis=0)


def apart(packed, heads):
    rows = packed.shape[0] - 2 * heads
    tail = packed[rows:, 0].astype(F32)
    return packed[:rows].astype(F32), tail[:heads] + tail[heads:]


def incoming_state(state, total, start, head_dim, later_use):
    place = lax.axis_index("ctx")
    pairs = lax.axis_size("ctx") // 2
    odd = place % 2 == 1
    z = place // 2
    heads = total.shape[0]
    half = heads // 2
    cut = half * head_dim
    keep = jnp.where(odd, state[cut:], state[:cut])
    keep_total = jnp.where(odd, total[half:], total[:half])
    give = jnp.where(odd, state[:cut], state[cut:])
    give_total = jnp.where(odd, total[:half], total[half:])
    got, got_total = apart(swap(with_total(give, give_total), "ctx", 1), half)

    def spread(v):
        return jnp.repeat(v, head_dim)[:, None]

    first = jnp.where(odd, got, keep)
    first_total = jnp.where(odd, got_total, keep_total)
    second = jnp.where(odd, keep, got)
    second_total = jnp.where(odd, keep_total, got_total)
    pair_state = spread(jnp.exp(-second_total)) * first + second
    pair_total = first_total + second_total
    packed = with_total(pair_state, pair_total)
    others = [apart(swap(packed, "ctx", 2 * d), half) for d in range(1, pairs)]
    states = [o[0] for o in others]
    totals = jnp.stack([o[1] for o in others])
    planes = jnp.stack([z ^ d for d in range(1, pairs)])
    between = (planes[None, :] > planes[:, None]) & (planes[None, :] < z)
    gap = jnp.sum(jnp.where(between[:, :, None], totals[None], 0.0), axis=1)
    weight = jnp.where((planes < z)[:, None], jnp.exp(-gap), 0.0)
    before = jnp.sum(jnp.where((planes < z)[:, None], totals, 0.0), axis=0)
    states, later_use = lax.optimization_barrier((states, later_use))
    own_start = jnp.where(odd, start[cut:], start[:cut])
    prefix = spread(jnp.exp(-before)) * own_start
    for i, s in enumerate(states):
        prefix = prefix + spread(weight[i]) * s
    later = spread(jnp.exp(-first_total)) * prefix + first
    mine = jnp.where(odd, later, prefix).astype(BF)
    other = swap(jnp.where(odd, prefix, later).astype(BF), "ctx", 1)
    return jnp.where(odd, other, mine), jnp.where(odd, mine, other), later_use


def mixer_rows(
    inputs, gate_input, b_proj, c_proj, step_size, decay_rate, skip_gain, start_state, later_use
):
    tok = inputs.shape[0]
    heads = step_size.shape[0]
    width = inputs.shape[1]
    head_dim = width // heads
    cumulative = jnp.cumsum(decay_rate, axis=1)
    total = cumulative[:, -1]

    def wide(v):
        return jnp.broadcast_to(v.T[:, :, None], (tok, heads, head_dim)).reshape(tok, width)

    x_local = inputs.astype(F32)
    ending = jnp.exp(-(total[:, None] - cumulative)) * step_size
    decayed = (x_local * wide(ending)).astype(BF)
    state = lax.dot_general(decayed, b_proj, (((0,), (0,)), ((), ())), preferred_element_type=F32)
    low, high, later_use = incoming_state(
        state, total, start_state.reshape(width, -1), head_dim, later_use
    )
    order = jnp.arange(tok, dtype=jnp.int32)
    causal = order[:, None] >= order[None, :]
    spread = jnp.where(causal[None], cumulative[:, :, None] - cumulative[:, None, :], 0.0)
    scores = lax.dot_general(c_proj, b_proj, (((1,), (1,)), ((), ())), preferred_element_type=F32)
    mixing = jnp.where(causal[None], jnp.exp(-spread), 0.0) * scores[None] * step_size[:, None, :]
    inside = jnp.einsum(
        "hts,shp->thp",
        mixing.astype(BF),
        inputs.reshape(tok, heads, head_dim),
        preferred_element_type=F32,
    ).reshape(tok, width)
    direct = inside + jnp.repeat(skip_gain, head_dim)[None, :] * x_local
    side = (((1,), (1,)), ((), ()))
    carried = jnp.concatenate(
        [
            lax.dot_general(c_proj, low, side, preferred_element_type=F32),
            lax.dot_general(c_proj, high, side, preferred_element_type=F32),
        ],
        axis=1,
    )
    ssm_out = direct + carried * wide(jnp.exp(-cumulative))
    return ssm_out * jax.nn.silu(gate_input.astype(F32)), later_use


def project_rows(gated, norm_gain, out_proj, neighbour_proj):
    n_exp = lax.axis_size("exp")
    n_ctx = lax.axis_size("ctx")
    me_exp = lax.axis_index("exp")
    me_ctx = lax.axis_index("ctx")
    tok, width = gated.shape
    quarter = tok // n_exp
    both = jnp.concatenate([out_proj, neighbour_proj], axis=1)
    squares = jnp.sum(gated * gated, axis=1)
    for flip in (1, 2):
        squares = squares + swap(squares, "exp", flip)
    own_squares = lax.dynamic_slice_in_dim(squares, me_exp * quarter, quarter, 0)
    scale = lax.rsqrt(own_squares / (width * n_exp) + eps_norm)

    rows = (gated * norm_gain[None, :]).astype(BF)
    rel = [0, 2, 1, 3]
    pieces = [lax.dynamic_slice_in_dim(rows, (me_exp ^ q) * quarter, quarter, 0) for q in rel]
    own_rows = jnp.concatenate(pieces)
    group = [h + y for h in range(0, n_ctx, 4) for y in (0, 1)]
    arrived = [own_rows] + [swap(own_rows, "ctx", r) for r in group[1:]]
    full = jnp.stack(arrived).reshape(len(group), n_exp, quarter, width)
    full = full.swapaxes(0, 1).reshape(-1, width)
    full, scale = lax.optimization_barrier((full, scale))
    partial = mm(full, both).astype(BF)
    for flip in (1, 2):
        cut = partial.shape[0] // 2
        got = swap(partial[cut:], "exp", flip)
        partial = (partial[:cut].astype(F32) + got.astype(F32)).astype(BF)
    partial = partial.reshape(len(group), quarter, -1)
    columns = out_proj.shape[1]
    blocks = [None] * n_ctx
    for i, r in enumerate(group):
        block = partial[i] if r == 0 else swap(partial[i], "ctx", r)
        blocks[r] = block[:, :columns]
        blocks[r ^ 2] = block[:, columns:]
    stacked = jnp.stack(blocks)
    mixed = jnp.concatenate(
        [lax.dynamic_index_in_dim(stacked, me_ctx ^ b, 0, False) for b in range(n_ctx)], axis=1
    )
    return mixed.astype(F32), scale


def pack_kernel(*refs):
    out = refs[-1]
    row = 0
    for piece in refs[:-1]:
        rows = piece.shape[0]
        out[row : row + rows, :] = piece[...]
        row += rows


def pack(pieces):
    rows = sum(p.shape[0] for p in pieces)
    width = pieces[0].shape[1]
    whole = pl.BlockSpec(memory_space=pltpu.VMEM)
    return pl.pallas_call(
        pack_kernel,
        out_shape=jax.ShapeDtypeStruct((rows, width), pieces[0].dtype),
        in_specs=[whole] * len(pieces),
        out_specs=whole,
        compiler_params=pltpu.CompilerParams(vmem_limit_bytes=32 * 1024 * 1024),
        cost_estimate=pl.CostEstimate(flops=0, bytes_accessed=4 * rows * width, transcendentals=0),
    )(*pieces)


def expert_kernel(
    own, mate, gate, up, down, pick, out_own, out_mate, rows, hidden, gu, dn, row_sem, gu_sem, dn_sem
):
    half = own.shape[0]
    model = gate.shape[0]
    tiles = gate.shape[1] // LANES
    down_tiles = model // DOWN_TILE
    row_copies = [
        pltpu.make_async_copy(own, rows.at[pl.ds(0, half)], row_sem.at[0]),
        pltpu.make_async_copy(mate, rows.at[pl.ds(half, half)], row_sem.at[1]),
    ]

    def gu_copies(j):
        at = pl.ds(pl.multiple_of(j * LANES, LANES), LANES)
        s = lax.rem(j, GU_SLOTS)
        return [
            pltpu.make_async_copy(gate.at[:, at], gu.at[s, :, pl.ds(0, LANES)], gu_sem.at[s, 0]),
            pltpu.make_async_copy(up.at[:, at], gu.at[s, :, pl.ds(LANES, LANES)], gu_sem.at[s, 1]),
        ]

    def dn_copy(j):
        at = pl.ds(pl.multiple_of(j * DOWN_TILE, DOWN_TILE), DOWN_TILE)
        s = lax.rem(j, DN_SLOTS)
        return pltpu.make_async_copy(down.at[:, at], dn.at[s], dn_sem.at[s])

    for c in row_copies:
        c.start()
    for j in range(GU_SLOTS - 1):
        for c in gu_copies(j):
            c.start()
    for c in row_copies:
        c.wait()

    def gate_up(j, carry):
        ahead = j + GU_SLOTS - 1
        for c in gu_copies(j):
            c.wait()

        @pl.when(ahead < tiles)
        def _():
            for c in gu_copies(ahead):
                c.start()

        @pl.when((ahead >= tiles) & (ahead - tiles < DN_SLOTS - 1))
        def _():
            dn_copy(ahead - tiles).start()

        both = mm(rows[:, :model], gu[lax.rem(j, GU_SLOTS)])
        gate_val = both[:, :LANES]
        act = gate_val / (1.0 + jnp.exp(-gate_val)) * both[:, LANES:]
        hidden[:, pl.ds(pl.multiple_of(j * LANES, LANES), LANES)] = act.astype(BF)
        return carry

    lax.fori_loop(0, tiles, gate_up, 0)
    weight = jnp.sum(rows[:, model:].astype(F32) * pick[...], axis=1, keepdims=True)

    def down_part(j, carry):
        dn_copy(j).wait()

        @pl.when(j + DN_SLOTS - 1 < down_tiles)
        def _():
            dn_copy(j + DN_SLOTS - 1).start()

        part = mm(hidden[...], dn[lax.rem(j, DN_SLOTS)]) * weight
        at = pl.ds(pl.multiple_of(j * DOWN_TILE, DOWN_TILE), DOWN_TILE)
        out_own[:, at] = part[:half].astype(BF)
        out_mate[:, at] = part[half:].astype(BF)
        return carry

    lax.fori_loop(0, down_tiles, down_part, 0)


def experts(own, mate, gate, up, down, pick):
    half, width = own.shape
    model, units = gate.shape
    out = jax.ShapeDtypeStruct((half, model), BF)
    whole = pl.BlockSpec(memory_space=pltpu.VMEM)
    anywhere = pl.BlockSpec(memory_space=pl.ANY)
    hbm = pl.BlockSpec(memory_space=pltpu.HBM)
    flops = 2 * 2 * half * model * units * 3
    moved = 2 * (3 * model * units + 8 * half * model)
    return pl.pallas_call(
        expert_kernel,
        out_shape=(out, out),
        in_specs=[anywhere] * 2 + [hbm] * 3 + [whole],
        out_specs=(whole, whole),
        scratch_shapes=[
            pltpu.VMEM((2 * half, width), BF),
            pltpu.VMEM((2 * half, units), BF),
            pltpu.VMEM((GU_SLOTS, model, 2 * LANES), BF),
            pltpu.VMEM((DN_SLOTS, units, DOWN_TILE), BF),
            pltpu.SemaphoreType.DMA((2,)),
            pltpu.SemaphoreType.DMA((GU_SLOTS, 2)),
            pltpu.SemaphoreType.DMA((DN_SLOTS,)),
        ],
        compiler_params=pltpu.CompilerParams(vmem_limit_bytes=48 * 1024 * 1024),
        cost_estimate=pl.CostEstimate(flops=flops, bytes_accessed=moved, transcendentals=2 * half * units),
    )(own, mate, gate, up, down, pick)


def together(values, others):
    return lax.optimization_barrier((tuple(values), others))


def across(x):
    n_ctx, n_exp = lax.axis_size("ctx"), lax.axis_size("exp")
    pairs = [
        (c * n_exp + e, (c ^ 1) * n_exp + (e ^ 2)) for c in range(n_ctx) for e in range(n_exp)
    ]
    return lax.ppermute(x, ("ctx", "exp"), pairs)


def summed(own, got, first, rows):
    last = first + rows
    return own[first:last].astype(F32) + got[first:last].astype(F32)


def plane_sums(own, got):
    size = own.shape[0] // 4
    to_x, to_y, to_xy = [summed(own, got, k * size, size).astype(BF) for k in (1, 2, 3)]
    return swap(to_x, "exp", 2), swap(to_y, "ctx", 1), across(to_xy)


def local(
    inputs,
    gate_input,
    b_proj,
    c_proj,
    step_size,
    decay_rate,
    skip_gain,
    start_state,
    norm_gain,
    out_proj,
    residual,
    moe_gain,
    w_gate,
    w_up,
    w_down,
    route_ids,
    route_gates,
):
    n_ctx = lax.axis_size("ctx")
    n_exp = lax.axis_size("exp")
    me_ctx = lax.axis_index("ctx")
    me_exp = lax.axis_index("exp")
    tok = inputs.shape[0]
    quarter = tok // n_exp
    pairs = n_ctx // 2
    named = route_ids[:, :, None] == jnp.arange(LANES // 2, dtype=jnp.int32)[None, None, :]
    weights = jnp.sum(jnp.where(named, route_gates[:, :, None], 0.0), axis=1)
    weights = lax.dynamic_slice_in_dim(weights, me_exp * quarter, quarter, 0)
    weights_high = weights.astype(BF)
    weights_low = (weights - weights_high.astype(F32)).astype(BF)
    lane = jnp.arange(LANES, dtype=jnp.int32)
    pick = (lane % (LANES // 2) == me_ctx // PAIR).astype(F32)[None, :]

    cut = out_proj.shape[0] // 2
    first_part = swap(out_proj[:cut], "ctx", 2)
    gated, second_part = mixer_rows(
        inputs, gate_input, b_proj, c_proj, step_size, decay_rate, skip_gain, start_state, out_proj[cut:]
    )
    neighbour_proj = jnp.concatenate([first_part, swap(second_part, "ctx", 2)])
    mixed, scale = project_rows(gated, norm_gain, out_proj, neighbour_proj)
    own_residual = lax.dynamic_slice_in_dim(residual, me_exp * quarter, quarter, 0)
    hidden = own_residual.astype(F32) + mixed * scale[:, None]
    moe_scale = lax.rsqrt(jnp.mean(hidden * hidden, axis=1, keepdims=True) + eps_norm)
    moe_in = (hidden * moe_scale * moe_gain[None, :]).astype(BF)

    payload = jnp.concatenate([moe_in, weights_high, weights_low], axis=1)
    order = [1] + list(range(pairs - 1, 1, -1)) + [0]
    count = len(order)
    by_distance = [payload]
    for d in range(1, pairs):
        low = d & -d
        by_distance.append(swap(by_distance[d - low], "ctx", 2 * low))
    planes = [by_distance[d] for d in order]
    near, rows, results, got, far_got = [], [], [], [], []

    def rest(stage):
        if 0 <= stage - 1 < count:
            got.append(swap(results[stage - 1][1], "exp", 1))
        if 0 <= stage - 2 < count:
            far_got.append(plane_sums(results[stage - 2][0], got[stage - 2]))

    def arrive(stage):
        if stage + 2 < count:
            piece = planes[stage + 2]
            near.append((swap(piece, "exp", 2), swap(piece, "ctx", 1), across(piece)))
        if 0 <= stage + 1 < count:
            own = pack((planes[stage + 1], *near[stage + 1]))
            rows.append((own, swap(own, "exp", 1)))

    for stage in (-2, -1):
        arrive(stage)
    for i in range(count):
        rest(i)
        arrive(i)
        beside = (got[-1:], far_got[-1:], rows[i + 1 :], near[i + 2 :])
        results.append(experts(*rows[i], w_gate[0], w_up[0], w_down[0], pick))
        results[i], beside = together(results[i], beside)
        got[-1:], far_got[-1:], rows[i + 1 :], near[i + 2 :] = beside
    for i in range(count, count + 2):
        rest(i)
    parts = [None] * pairs
    for i, d in enumerate(order):
        parts[d] = summed(results[i][0], got[i], 0, quarter)
        for v in far_got[i]:
            parts[d] = parts[d] + v.astype(F32)
    for d in sorted(range(1, pairs), key=lambda d: (-bin(d).count("1"), d)):
        low = d & -d
        parts[d - low] = parts[d - low] + swap(parts[d].astype(BF), "ctx", 2 * low).astype(F32)
    return (hidden + parts[0]).astype(BF)


def solution(mesh):
    in_specs = (
        P("ctx", "exp"),
        P("ctx", "exp"),
        P("ctx", None),
        P("ctx", None),
        P("exp", "ctx"),
        P("exp", "ctx"),
        P("exp"),
        P("exp", None, None),
        P("exp"),
        P("exp", "ctx"),
        P("ctx", None),
        P(),
        P("ctx", None, "exp"),
        P("ctx", None, "exp"),
        P("ctx", "exp", None),
        P("ctx", None),
        P("ctx", None),
    )
    out_specs = P(("ctx", "exp"), None)
    return jax.shard_map(local, mesh=mesh, in_specs=in_specs, out_specs=out_specs, check_vma=False)
```

```python
import jax
import jax.numpy as jnp
from jax import lax
from jax.experimental import pallas as pl
from jax.experimental.pallas import tpu as pltpu
from jax.sharding import PartitionSpec as P

PAIR = 2
eps_norm = 1e-05
BF = jnp.bfloat16
F32 = jnp.float32
LANES = 128
DOWN_TILE = 1024
GU_SLOTS = 4
DN_SLOTS = 3


def swap(x, axis, flip):
    size = lax.axis_size(axis)
    return lax.ppermute(x, axis, [(i, i ^ flip) for i in range(size)])


def mm(a, b):
    return jnp.dot(a, b, preferred_element_type=F32)


def split_total(total):
    high = total.astype(BF)
    low = (total - high.astype(F32)).astype(BF)
    both = jnp.concatenate([high, low])
    return jnp.broadcast_to(both[:, None], (both.shape[0], 128))


def with_total(state, total):
    return jnp.concatenate([state.astype(BF), split_total(total)], axis=0)


def apart(packed, heads):
    rows = packed.shape[0] - 2 * heads
    tail = packed[rows:, 0].astype(F32)
    return packed[:rows].astype(F32), tail[:heads] + tail[heads:]


def incoming_state(state, total, start, head_dim, later_use):
    place = lax.axis_index("ctx")
    pairs = lax.axis_size("ctx") // 2
    odd = place % 2 == 1
    z = place // 2
    heads = total.shape[0]
    half = heads // 2
    cut = half * head_dim
    keep = jnp.where(odd, state[cut:], state[:cut])
    keep_total = jnp.where(odd, total[half:], total[:half])
    give = jnp.where(odd, state[:cut], state[cut:])
    give_total = jnp.where(odd, total[:half], total[half:])
    got, got_total = apart(swap(with_total(give, give_total), "ctx", 1), half)

    def spread(v):
        return jnp.repeat(v, head_dim)[:, None]

    first = jnp.where(odd, got, keep)
    first_total = jnp.where(odd, got_total, keep_total)
    second = jnp.where(odd, keep, got)
    second_total = jnp.where(odd, keep_total, got_total)
    pair_state = spread(jnp.exp(-second_total)) * first + second
    pair_total = first_total + second_total
    packed = with_total(pair_state, pair_total)
    others = [apart(swap(packed, "ctx", 2 * d), half) for d in range(1, pairs)]
    states = [o[0] for o in others]
    totals = jnp.stack([o[1] for o in others])
    planes = jnp.stack([z ^ d for d in range(1, pairs)])
    between = (planes[None, :] > planes[:, None]) & (planes[None, :] < z)
    gap = jnp.sum(jnp.where(between[:, :, None], totals[None], 0.0), axis=1)
    weight = jnp.where((planes < z)[:, None], jnp.exp(-gap), 0.0)
    before = jnp.sum(jnp.where((planes < z)[:, None], totals, 0.0), axis=0)
    states, later_use = lax.optimization_barrier((states, later_use))
    own_start = jnp.where(odd, start[cut:], start[:cut])
    prefix = spread(jnp.exp(-before)) * own_start
    for i, s in enumerate(states):
        prefix = prefix + spread(weight[i]) * s
    later = spread(jnp.exp(-first_total)) * prefix + first
    mine = jnp.where(odd, later, prefix).astype(BF)
    other = swap(jnp.where(odd, prefix, later).astype(BF), "ctx", 1)
    return jnp.where(odd, other, mine), jnp.where(odd, mine, other), later_use


def mixer_rows(
    inputs, gate_input, b_proj, c_proj, step_size, decay_rate, skip_gain, start_state, later_use
):
    tok = inputs.shape[0]
    heads = step_size.shape[0]
    width = inputs.shape[1]
    head_dim = width // heads
    cumulative = jnp.cumsum(decay_rate, axis=1)
    total = cumulative[:, -1]

    def wide(v):
        return jnp.broadcast_to(v.T[:, :, None], (tok, heads, head_dim)).reshape(tok, width)

    x_local = inputs.astype(F32)
    ending = jnp.exp(-(total[:, None] - cumulative)) * step_size
    decayed = (x_local * wide(ending)).astype(BF)
    state = lax.dot_general(decayed, b_proj, (((0,), (0,)), ((), ())), preferred_element_type=F32)
    low, high, later_use = incoming_state(
        state, total, start_state.reshape(width, -1), head_dim, later_use
    )
    order = jnp.arange(tok, dtype=jnp.int32)
    causal = order[:, None] >= order[None, :]
    spread = jnp.where(causal[None], cumulative[:, :, None] - cumulative[:, None, :], 0.0)
    scores = lax.dot_general(c_proj, b_proj, (((1,), (1,)), ((), ())), preferred_element_type=F32)
    mixing = jnp.where(causal[None], jnp.exp(-spread), 0.0) * scores[None] * step_size[:, None, :]
    inside = jnp.einsum(
        "hts,shp->thp",
        mixing.astype(BF),
        inputs.reshape(tok, heads, head_dim),
        preferred_element_type=F32,
    ).reshape(tok, width)
    direct = inside + jnp.repeat(skip_gain, head_dim)[None, :] * x_local
    side = (((1,), (1,)), ((), ()))
    carried = jnp.concatenate(
        [
            lax.dot_general(c_proj, low, side, preferred_element_type=F32),
            lax.dot_general(c_proj, high, side, preferred_element_type=F32),
        ],
        axis=1,
    )
    ssm_out = direct + carried * wide(jnp.exp(-cumulative))
    return ssm_out * jax.nn.silu(gate_input.astype(F32)), later_use


def project_rows(gated, norm_gain, out_proj, neighbour_proj):
    n_exp = lax.axis_size("exp")
    n_ctx = lax.axis_size("ctx")
    me_exp = lax.axis_index("exp")
    me_ctx = lax.axis_index("ctx")
    tok, width = gated.shape
    quarter = tok // n_exp
    both = jnp.concatenate([out_proj, neighbour_proj], axis=1)
    squares = jnp.sum(gated * gated, axis=1)
    rows = (gated * norm_gain[None, :]).astype(BF)
    rel = [0, 2, 1, 3]
    pieces = [lax.dynamic_slice_in_dim(rows, (me_exp ^ q) * quarter, quarter, 0) for q in rel]
    own_rows = jnp.concatenate(pieces)
    group = [h + y for h in range(0, n_ctx, 4) for y in (0, 1)]
    arrived = [own_rows] + [swap(own_rows, "ctx", r) for r in group[1:]]
    squares, arrived[1] = lax.optimization_barrier((squares, arrived[1]))
    for flip in (1, 2):
        squares = squares + swap(squares, "exp", flip)
    own_squares = lax.dynamic_slice_in_dim(squares, me_exp * quarter, quarter, 0)
    scale = lax.rsqrt(own_squares / (width * n_exp) + eps_norm)
    full = jnp.stack(arrived).reshape(len(group), n_exp, quarter, width)
    full = full.swapaxes(0, 1).reshape(-1, width)
    full, scale = lax.optimization_barrier((full, scale))
    partial = mm(full, both).astype(BF)
    for flip in (1, 2):
        cut = partial.shape[0] // 2
        got = swap(partial[cut:], "exp", flip)
        partial = (partial[:cut].astype(F32) + got.astype(F32)).astype(BF)
    partial = partial.reshape(len(group), quarter, -1)
    columns = out_proj.shape[1]
    blocks = [None] * n_ctx
    for i, r in enumerate(group):
        block = partial[i] if r == 0 else swap(partial[i], "ctx", r)
        blocks[r] = block[:, :columns]
        blocks[r ^ 2] = block[:, columns:]
    stacked = jnp.stack(blocks)
    mixed = jnp.concatenate(
        [lax.dynamic_index_in_dim(stacked, me_ctx ^ b, 0, False) for b in range(n_ctx)], axis=1
    )
    return mixed.astype(F32), scale


def pack_kernel(*refs):
    out = refs[-1]
    row = 0
    for piece in refs[:-1]:
        rows = piece.shape[0]
        out[row : row + rows, :] = piece[...]
        row += rows


def pack(pieces):
    rows = sum(p.shape[0] for p in pieces)
    width = pieces[0].shape[1]
    whole = pl.BlockSpec(memory_space=pltpu.VMEM)
    return pl.pallas_call(
        pack_kernel,
        out_shape=jax.ShapeDtypeStruct((rows, width), pieces[0].dtype),
        in_specs=[whole] * len(pieces),
        out_specs=whole,
        compiler_params=pltpu.CompilerParams(vmem_limit_bytes=32 * 1024 * 1024),
        cost_estimate=pl.CostEstimate(flops=0, bytes_accessed=4 * rows * width, transcendentals=0),
    )(*pieces)


def expert_kernel(
    own, mate, gate, up, down, pick, out_own, out_mate, rows, hidden, gu, dn, row_sem, gu_sem, dn_sem
):
    half = own.shape[0]
    model = gate.shape[0]
    tiles = gate.shape[1] // LANES
    down_tiles = model // DOWN_TILE
    row_copies = [
        pltpu.make_async_copy(own, rows.at[pl.ds(0, half)], row_sem.at[0]),
        pltpu.make_async_copy(mate, rows.at[pl.ds(half, half)], row_sem.at[1]),
    ]

    def gu_copies(j):
        at = pl.ds(pl.multiple_of(j * LANES, LANES), LANES)
        s = lax.rem(j, GU_SLOTS)
        return [
            pltpu.make_async_copy(gate.at[:, at], gu.at[s, :, pl.ds(0, LANES)], gu_sem.at[s, 0]),
            pltpu.make_async_copy(up.at[:, at], gu.at[s, :, pl.ds(LANES, LANES)], gu_sem.at[s, 1]),
        ]

    def dn_copy(j):
        at = pl.ds(pl.multiple_of(j * DOWN_TILE, DOWN_TILE), DOWN_TILE)
        s = lax.rem(j, DN_SLOTS)
        return pltpu.make_async_copy(down.at[:, at], dn.at[s], dn_sem.at[s])

    for c in row_copies:
        c.start()
    for j in range(GU_SLOTS - 1):
        for c in gu_copies(j):
            c.start()
    for c in row_copies:
        c.wait()

    def gate_up(j, carry):
        ahead = j + GU_SLOTS - 1
        for c in gu_copies(j):
            c.wait()

        @pl.when(ahead < tiles)
        def _():
            for c in gu_copies(ahead):
                c.start()

        @pl.when((ahead >= tiles) & (ahead - tiles < DN_SLOTS - 1))
        def _():
            dn_copy(ahead - tiles).start()

        both = mm(rows[:, :model], gu[lax.rem(j, GU_SLOTS)])
        gate_val = both[:, :LANES]
        act = gate_val / (1.0 + jnp.exp(-gate_val)) * both[:, LANES:]
        hidden[:, pl.ds(pl.multiple_of(j * LANES, LANES), LANES)] = act.astype(BF)
        return carry

    lax.fori_loop(0, tiles, gate_up, 0)
    weight = jnp.sum(rows[:, model:].astype(F32) * pick[...], axis=1, keepdims=True)

    def down_part(j, carry):
        dn_copy(j).wait()

        @pl.when(j + DN_SLOTS - 1 < down_tiles)
        def _():
            dn_copy(j + DN_SLOTS - 1).start()

        part = mm(hidden[...], dn[lax.rem(j, DN_SLOTS)]) * weight
        at = pl.ds(pl.multiple_of(j * DOWN_TILE, DOWN_TILE), DOWN_TILE)
        out_own[:, at] = part[:half].astype(BF)
        out_mate[:, at] = part[half:].astype(BF)
        return carry

    lax.fori_loop(0, down_tiles, down_part, 0)


def experts(own, mate, gate, up, down, pick):
    half, width = own.shape
    model, units = gate.shape
    out = jax.ShapeDtypeStruct((half, model), BF)
    whole = pl.BlockSpec(memory_space=pltpu.VMEM)
    anywhere = pl.BlockSpec(memory_space=pl.ANY)
    hbm = pl.BlockSpec(memory_space=pltpu.HBM)
    flops = 2 * 2 * half * model * units * 3
    moved = 2 * (3 * model * units + 8 * half * model)
    return pl.pallas_call(
        expert_kernel,
        out_shape=(out, out),
        in_specs=[anywhere] * 2 + [hbm] * 3 + [whole],
        out_specs=(whole, whole),
        scratch_shapes=[
            pltpu.VMEM((2 * half, width), BF),
            pltpu.VMEM((2 * half, units), BF),
            pltpu.VMEM((GU_SLOTS, model, 2 * LANES), BF),
            pltpu.VMEM((DN_SLOTS, units, DOWN_TILE), BF),
            pltpu.SemaphoreType.DMA((2,)),
            pltpu.SemaphoreType.DMA((GU_SLOTS, 2)),
            pltpu.SemaphoreType.DMA((DN_SLOTS,)),
        ],
        compiler_params=pltpu.CompilerParams(vmem_limit_bytes=48 * 1024 * 1024),
        cost_estimate=pl.CostEstimate(flops=flops, bytes_accessed=moved, transcendentals=2 * half * units),
    )(own, mate, gate, up, down, pick)


def together(values, others):
    return lax.optimization_barrier((tuple(values), others))


def across(x):
    n_ctx, n_exp = lax.axis_size("ctx"), lax.axis_size("exp")
    pairs = [
        (c * n_exp + e, (c ^ 1) * n_exp + (e ^ 2)) for c in range(n_ctx) for e in range(n_exp)
    ]
    return lax.ppermute(x, ("ctx", "exp"), pairs)


def summed(own, got, first, rows):
    last = first + rows
    return own[first:last].astype(F32) + got[first:last].astype(F32)


def plane_sums(own, got):
    size = own.shape[0] // 4
    to_x, to_y, to_xy = [summed(own, got, k * size, size).astype(BF) for k in (1, 2, 3)]
    return swap(to_x, "exp", 2), swap(to_y, "ctx", 1), across(to_xy)


def local(
    inputs,
    gate_input,
    b_proj,
    c_proj,
    step_size,
    decay_rate,
    skip_gain,
    start_state,
    norm_gain,
    out_proj,
    residual,
    moe_gain,
    w_gate,
    w_up,
    w_down,
    route_ids,
    route_gates,
):
    n_ctx = lax.axis_size("ctx")
    n_exp = lax.axis_size("exp")
    me_ctx = lax.axis_index("ctx")
    me_exp = lax.axis_index("exp")
    tok = inputs.shape[0]
    quarter = tok // n_exp
    pairs = n_ctx // 2
    named = route_ids[:, :, None] == jnp.arange(LANES // 2, dtype=jnp.int32)[None, None, :]
    weights = jnp.sum(jnp.where(named, route_gates[:, :, None], 0.0), axis=1)
    weights = lax.dynamic_slice_in_dim(weights, me_exp * quarter, quarter, 0)
    weights_high = weights.astype(BF)
    weights_low = (weights - weights_high.astype(F32)).astype(BF)
    lane = jnp.arange(LANES, dtype=jnp.int32)
    pick = (lane % (LANES // 2) == me_ctx // PAIR).astype(F32)[None, :]

    cut = out_proj.shape[0] // 4
    two_parts = (swap(out_proj[:cut], "ctx", 2), out_proj[cut:])
    gated, (first_part, second_part) = mixer_rows(
        inputs, gate_input, b_proj, c_proj, step_size, decay_rate, skip_gain, start_state, two_parts
    )
    neighbour_proj = jnp.concatenate([first_part, swap(second_part, "ctx", 2)])
    mixed, scale = project_rows(gated, norm_gain, out_proj, neighbour_proj)
    own_residual = lax.dynamic_slice_in_dim(residual, me_exp * quarter, quarter, 0)
    hidden = own_residual.astype(F32) + mixed * scale[:, None]
    moe_scale = lax.rsqrt(jnp.mean(hidden * hidden, axis=1, keepdims=True) + eps_norm)
    moe_in = (hidden * moe_scale * moe_gain[None, :]).astype(BF)

    payload = jnp.concatenate([moe_in, weights_high, weights_low], axis=1)
    order = [0] + list(range(2, pairs)) + [1]
    count = len(order)
    by_distance = [payload]
    for d in range(1, pairs):
        low = d & -d
        by_distance.append(swap(by_distance[d - low], "ctx", 2 * low))
    planes = [by_distance[d] for d in order]
    near, rows, results, got, far_got, parts = [], [], [], [], [], []

    def neighbours(piece):
        return swap(piece, "exp", 2), swap(piece, "ctx", 1), across(piece)

    def core(k):
        if 0 <= k < count:
            got.append(swap(results[k][1], "exp", 1))

    def spread(k):
        if 0 <= k < count:
            far_got.append(plane_sums(results[k][0], got[k]))

    def back(k):
        if 0 <= k < count:
            part = summed(results[k][0], got[k], 0, quarter)
            for v in far_got[k]:
                part = part + v.astype(F32)
            d = order[k]
            parts.append(part if d == 0 else swap(part.astype(BF), "ctx", 2 * d))

    def bring(k):
        if k < count:
            near.append(neighbours(planes[k]))

    def ready(k):
        if k < count:
            own = pack((planes[k], *near[k]))
            rows.append((own, swap(own, "exp", 1)))

    bring(0)
    near[0], planes[1] = together(near[0], planes[1])
    for i in range(count):
        ready(i)
        core(i - 1)
        spread(i - 2)
        back(i - 3)
        bring(i + 1)
        beside = (got[-1:], far_got[-1:], parts[-1:], near[i + 1 :], planes[i + 2 :])
        results.append(experts(*rows[i], w_gate[0], w_up[0], w_down[0], pick))
        results[i], beside = together(results[i], beside)
        got[-1:], far_got[-1:], parts[-1:], near[i + 1 :], planes[i + 2 :] = beside
    core(count - 1)
    spread(count - 2)
    back(count - 3)
    spread(count - 1)
    back(count - 2)
    back(count - 1)
    for part in parts:
        hidden = hidden + part.astype(F32)
    return hidden.astype(BF)


def solution(mesh):
    in_specs = (
        P("ctx", "exp"),
        P("ctx", "exp"),
        P("ctx", None),
        P("ctx", None),
        P("exp", "ctx"),
        P("exp", "ctx"),
        P("exp"),
        P("exp", None, None),
        P("exp"),
        P("exp", "ctx"),
        P("ctx", None),
        P(),
        P("ctx", None, "exp"),
        P("ctx", None, "exp"),
        P("ctx", "exp", None),
        P("ctx", None),
        P("ctx", None),
    )
    out_specs = P(("ctx", "exp"), None)
    return jax.shard_map(local, mesh=mesh, in_specs=in_specs, out_specs=out_specs, check_vma=False)
```

```python
import jax
import jax.numpy as jnp
from jax import lax
from jax.experimental import pallas as pl
from jax.experimental.pallas import tpu as pltpu
from jax.sharding import PartitionSpec as P

PAIR = 2
eps_norm = 1e-05
BF = jnp.bfloat16
F32 = jnp.float32
LANES = 128
DOWN_TILE = 1024
GU_SLOTS = 4
DN_SLOTS = 3


def swap(x, axis, flip):
    size = lax.axis_size(axis)
    return lax.ppermute(x, axis, [(i, i ^ flip) for i in range(size)])


def mm(a, b):
    return jnp.dot(a, b, preferred_element_type=F32)


def split_total(total):
    high = total.astype(BF)
    low = (total - high.astype(F32)).astype(BF)
    both = jnp.concatenate([high, low])
    return jnp.broadcast_to(both[:, None], (both.shape[0], 128))


def with_total(state, total):
    return jnp.concatenate([state.astype(BF), split_total(total)], axis=0)


def apart(packed, heads):
    rows = packed.shape[0] - 2 * heads
    tail = packed[rows:, 0].astype(F32)
    return packed[:rows].astype(F32), tail[:heads] + tail[heads:]


def incoming_state(state, total, start, head_dim, later_use):
    place = lax.axis_index("ctx")
    pairs = lax.axis_size("ctx") // 2
    odd = place % 2 == 1
    z = place // 2
    heads = total.shape[0]
    half = heads // 2
    cut = half * head_dim
    keep = jnp.where(odd, state[cut:], state[:cut])
    keep_total = jnp.where(odd, total[half:], total[:half])
    give = jnp.where(odd, state[:cut], state[cut:])
    give_total = jnp.where(odd, total[:half], total[half:])
    got, got_total = apart(swap(with_total(give, give_total), "ctx", 1), half)

    def spread(v):
        return jnp.repeat(v, head_dim)[:, None]

    first = jnp.where(odd, got, keep)
    first_total = jnp.where(odd, got_total, keep_total)
    second = jnp.where(odd, keep, got)
    second_total = jnp.where(odd, keep_total, got_total)
    pair_state = spread(jnp.exp(-second_total)) * first + second
    pair_total = first_total + second_total
    packed = with_total(pair_state, pair_total)
    others = [apart(swap(packed, "ctx", 2 * d), half) for d in range(1, pairs)]
    states = [o[0] for o in others]
    totals = jnp.stack([o[1] for o in others])
    planes = jnp.stack([z ^ d for d in range(1, pairs)])
    between = (planes[None, :] > planes[:, None]) & (planes[None, :] < z)
    gap = jnp.sum(jnp.where(between[:, :, None], totals[None], 0.0), axis=1)
    weight = jnp.where((planes < z)[:, None], jnp.exp(-gap), 0.0)
    before = jnp.sum(jnp.where((planes < z)[:, None], totals, 0.0), axis=0)
    states, later_use = lax.optimization_barrier((states, later_use))
    own_start = jnp.where(odd, start[cut:], start[:cut])
    prefix = spread(jnp.exp(-before)) * own_start
    for i, s in enumerate(states):
        prefix = prefix + spread(weight[i]) * s
    later = spread(jnp.exp(-first_total)) * prefix + first
    mine = jnp.where(odd, later, prefix).astype(BF)
    other = swap(jnp.where(odd, prefix, later).astype(BF), "ctx", 1)
    return jnp.where(odd, other, mine), jnp.where(odd, mine, other), later_use


def mixer_rows(
    inputs, gate_input, b_proj, c_proj, step_size, decay_rate, skip_gain, start_state, later_use
):
    tok = inputs.shape[0]
    heads = step_size.shape[0]
    width = inputs.shape[1]
    head_dim = width // heads
    cumulative = jnp.cumsum(decay_rate, axis=1)
    total = cumulative[:, -1]

    def wide(v):
        return jnp.broadcast_to(v.T[:, :, None], (tok, heads, head_dim)).reshape(tok, width)

    x_local = inputs.astype(F32)
    ending = jnp.exp(-(total[:, None] - cumulative)) * step_size
    decayed = (x_local * wide(ending)).astype(BF)
    state = lax.dot_general(decayed, b_proj, (((0,), (0,)), ((), ())), preferred_element_type=F32)
    low, high, later_use = incoming_state(
        state, total, start_state.reshape(width, -1), head_dim, later_use
    )
    order = jnp.arange(tok, dtype=jnp.int32)
    causal = order[:, None] >= order[None, :]
    spread = jnp.where(causal[None], cumulative[:, :, None] - cumulative[:, None, :], 0.0)
    scores = lax.dot_general(c_proj, b_proj, (((1,), (1,)), ((), ())), preferred_element_type=F32)
    mixing = jnp.where(causal[None], jnp.exp(-spread), 0.0) * scores[None] * step_size[:, None, :]
    inside = jnp.einsum(
        "hts,shp->thp",
        mixing.astype(BF),
        inputs.reshape(tok, heads, head_dim),
        preferred_element_type=F32,
    ).reshape(tok, width)
    direct = inside + jnp.repeat(skip_gain, head_dim)[None, :] * x_local
    side = (((1,), (1,)), ((), ()))
    carried = jnp.concatenate(
        [
            lax.dot_general(c_proj, low, side, preferred_element_type=F32),
            lax.dot_general(c_proj, high, side, preferred_element_type=F32),
        ],
        axis=1,
    )
    ssm_out = direct + carried * wide(jnp.exp(-cumulative))
    return ssm_out * jax.nn.silu(gate_input.astype(F32)), later_use


def project_rows(gated, norm_gain, out_proj, neighbour_proj):
    n_exp = lax.axis_size("exp")
    n_ctx = lax.axis_size("ctx")
    me_exp = lax.axis_index("exp")
    me_ctx = lax.axis_index("ctx")
    tok, width = gated.shape
    quarter = tok // n_exp
    both = jnp.concatenate([out_proj, neighbour_proj], axis=1)
    squares = jnp.sum(gated * gated, axis=1)
    rows = (gated * norm_gain[None, :]).astype(BF)
    rel = [0, 2, 1, 3]
    pieces = [lax.dynamic_slice_in_dim(rows, (me_exp ^ q) * quarter, quarter, 0) for q in rel]
    own_rows = jnp.concatenate(pieces)
    group = [h + y for h in range(0, n_ctx, 4) for y in (0, 1)]
    arrived = [own_rows] + [swap(own_rows, "ctx", r) for r in group[1:]]
    squares, arrived[1] = lax.optimization_barrier((squares, arrived[1]))
    for flip in (1, 2):
        squares = squares + swap(squares, "exp", flip)
    own_squares = lax.dynamic_slice_in_dim(squares, me_exp * quarter, quarter, 0)
    scale = lax.rsqrt(own_squares / (width * n_exp) + eps_norm)
    full = jnp.stack(arrived).reshape(len(group), n_exp, quarter, width)
    full = full.swapaxes(0, 1).reshape(-1, width)
    full, scale = lax.optimization_barrier((full, scale))
    partial = mm(full, both).astype(BF)
    for flip in (1, 2):
        cut = partial.shape[0] // 2
        got = swap(partial[cut:], "exp", flip)
        partial = (partial[:cut].astype(F32) + got.astype(F32)).astype(BF)
    partial = partial.reshape(len(group), quarter, -1)
    columns = out_proj.shape[1]
    blocks = [None] * n_ctx
    for i, r in enumerate(group):
        block = partial[i] if r == 0 else swap(partial[i], "ctx", r)
        blocks[r] = block[:, :columns]
        blocks[r ^ 2] = block[:, columns:]
    stacked = jnp.stack(blocks)
    mixed = jnp.concatenate(
        [lax.dynamic_index_in_dim(stacked, me_ctx ^ b, 0, False) for b in range(n_ctx)], axis=1
    )
    return mixed.astype(F32), scale


def pack_kernel(*refs):
    out = refs[-1]
    row = 0
    for piece in refs[:-1]:
        rows = piece.shape[0]
        out[row : row + rows, :] = piece[...]
        row += rows


def pack(pieces):
    rows = sum(p.shape[0] for p in pieces)
    width = pieces[0].shape[1]
    whole = pl.BlockSpec(memory_space=pltpu.VMEM)
    return pl.pallas_call(
        pack_kernel,
        out_shape=jax.ShapeDtypeStruct((rows, width), pieces[0].dtype),
        in_specs=[whole] * len(pieces),
        out_specs=whole,
        compiler_params=pltpu.CompilerParams(vmem_limit_bytes=32 * 1024 * 1024),
        cost_estimate=pl.CostEstimate(flops=0, bytes_accessed=4 * rows * width, transcendentals=0),
    )(*pieces)


def expert_kernel(
    own, mate, gate, up, down, pick, out_own, out_mate, rows, hidden, gu, dn, row_sem, gu_sem, dn_sem
):
    half = own.shape[0]
    model = gate.shape[0]
    tiles = gate.shape[1] // LANES
    down_tiles = model // DOWN_TILE
    row_copies = [
        pltpu.make_async_copy(own, rows.at[pl.ds(0, half)], row_sem.at[0]),
        pltpu.make_async_copy(mate, rows.at[pl.ds(half, half)], row_sem.at[1]),
    ]

    def gu_copies(j):
        at = pl.ds(pl.multiple_of(j * LANES, LANES), LANES)
        s = lax.rem(j, GU_SLOTS)
        return [
            pltpu.make_async_copy(gate.at[:, at], gu.at[s, :, pl.ds(0, LANES)], gu_sem.at[s, 0]),
            pltpu.make_async_copy(up.at[:, at], gu.at[s, :, pl.ds(LANES, LANES)], gu_sem.at[s, 1]),
        ]

    def dn_copy(j):
        at = pl.ds(pl.multiple_of(j * DOWN_TILE, DOWN_TILE), DOWN_TILE)
        s = lax.rem(j, DN_SLOTS)
        return pltpu.make_async_copy(down.at[:, at], dn.at[s], dn_sem.at[s])

    for c in row_copies:
        c.start()
    for j in range(GU_SLOTS - 1):
        for c in gu_copies(j):
            c.start()
    for c in row_copies:
        c.wait()

    def gate_up(j, carry):
        ahead = j + GU_SLOTS - 1
        for c in gu_copies(j):
            c.wait()

        @pl.when(ahead < tiles)
        def _():
            for c in gu_copies(ahead):
                c.start()

        @pl.when((ahead >= tiles) & (ahead - tiles < DN_SLOTS - 1))
        def _():
            dn_copy(ahead - tiles).start()

        both = mm(rows[:, :model], gu[lax.rem(j, GU_SLOTS)])
        gate_val = both[:, :LANES]
        act = gate_val / (1.0 + jnp.exp(-gate_val)) * both[:, LANES:]
        hidden[:, pl.ds(pl.multiple_of(j * LANES, LANES), LANES)] = act.astype(BF)
        return carry

    lax.fori_loop(0, tiles, gate_up, 0)
    weight = jnp.sum(rows[:, model:].astype(F32) * pick[...], axis=1, keepdims=True)

    def down_part(j, carry):
        dn_copy(j).wait()

        @pl.when(j + DN_SLOTS - 1 < down_tiles)
        def _():
            dn_copy(j + DN_SLOTS - 1).start()

        part = mm(hidden[...], dn[lax.rem(j, DN_SLOTS)]) * weight
        at = pl.ds(pl.multiple_of(j * DOWN_TILE, DOWN_TILE), DOWN_TILE)
        out_own[:, at] = part[:half].astype(BF)
        out_mate[:, at] = part[half:].astype(BF)
        return carry

    lax.fori_loop(0, down_tiles, down_part, 0)


def experts(own, mate, gate, up, down, pick):
    half, width = own.shape
    model, units = gate.shape
    out = jax.ShapeDtypeStruct((half, model), BF)
    whole = pl.BlockSpec(memory_space=pltpu.VMEM)
    anywhere = pl.BlockSpec(memory_space=pl.ANY)
    hbm = pl.BlockSpec(memory_space=pltpu.HBM)
    flops = 2 * 2 * half * model * units * 3
    moved = 2 * (3 * model * units + 8 * half * model)
    return pl.pallas_call(
        expert_kernel,
        out_shape=(out, out),
        in_specs=[anywhere] * 2 + [hbm] * 3 + [whole],
        out_specs=(whole, whole),
        scratch_shapes=[
            pltpu.VMEM((2 * half, width), BF),
            pltpu.VMEM((2 * half, units), BF),
            pltpu.VMEM((GU_SLOTS, model, 2 * LANES), BF),
            pltpu.VMEM((DN_SLOTS, units, DOWN_TILE), BF),
            pltpu.SemaphoreType.DMA((2,)),
            pltpu.SemaphoreType.DMA((GU_SLOTS, 2)),
            pltpu.SemaphoreType.DMA((DN_SLOTS,)),
        ],
        compiler_params=pltpu.CompilerParams(vmem_limit_bytes=48 * 1024 * 1024),
        cost_estimate=pl.CostEstimate(flops=flops, bytes_accessed=moved, transcendentals=2 * half * units),
    )(own, mate, gate, up, down, pick)


def together(values, others):
    return lax.optimization_barrier((tuple(values), others))


def across(x):
    n_ctx, n_exp = lax.axis_size("ctx"), lax.axis_size("exp")
    pairs = [
        (c * n_exp + e, (c ^ 1) * n_exp + (e ^ 2)) for c in range(n_ctx) for e in range(n_exp)
    ]
    return lax.ppermute(x, ("ctx", "exp"), pairs)


def summed(own, got, first, rows):
    last = first + rows
    return own[first:last].astype(F32) + got[first:last].astype(F32)


def plane_sums(own, got, others):
    size = own.shape[0] // 4
    sums = [summed(own, got, k * size, size).astype(BF) for k in (1, 2, 3)]
    (to_x,), others = together(sums[:1], others)
    return (swap(to_x, "exp", 2), swap(sums[1], "ctx", 1), across(sums[2])), others


def local(
    inputs,
    gate_input,
    b_proj,
    c_proj,
    step_size,
    decay_rate,
    skip_gain,
    start_state,
    norm_gain,
    out_proj,
    residual,
    moe_gain,
    w_gate,
    w_up,
    w_down,
    route_ids,
    route_gates,
):
    n_ctx = lax.axis_size("ctx")
    n_exp = lax.axis_size("exp")
    me_ctx = lax.axis_index("ctx")
    me_exp = lax.axis_index("exp")
    tok = inputs.shape[0]
    quarter = tok // n_exp
    pairs = n_ctx // 2
    named = route_ids[:, :, None] == jnp.arange(LANES // 2, dtype=jnp.int32)[None, None, :]
    weights = jnp.sum(jnp.where(named, route_gates[:, :, None], 0.0), axis=1)
    weights = lax.dynamic_slice_in_dim(weights, me_exp * quarter, quarter, 0)
    weights_high = weights.astype(BF)
    weights_low = (weights - weights_high.astype(F32)).astype(BF)
    lane = jnp.arange(LANES, dtype=jnp.int32)
    pick = (lane % (LANES // 2) == me_ctx // PAIR).astype(F32)[None, :]

    cut = out_proj.shape[0] // 4
    two_parts = (swap(out_proj[:cut], "ctx", 2), out_proj[cut:])
    gated, (first_part, second_part) = mixer_rows(
        inputs, gate_input, b_proj, c_proj, step_size, decay_rate, skip_gain, start_state, two_parts
    )
    neighbour_proj = jnp.concatenate([first_part, swap(second_part, "ctx", 2)])
    mixed, scale = project_rows(gated, norm_gain, out_proj, neighbour_proj)
    own_residual = lax.dynamic_slice_in_dim(residual, me_exp * quarter, quarter, 0)
    hidden = own_residual.astype(F32) + mixed * scale[:, None]
    moe_scale = lax.rsqrt(jnp.mean(hidden * hidden, axis=1, keepdims=True) + eps_norm)
    moe_in = (hidden * moe_scale * moe_gain[None, :]).astype(BF)

    payload = jnp.concatenate([moe_in, weights_high, weights_low], axis=1)
    order = [0] + list(range(2, pairs)) + [1]
    count = len(order)
    by_distance = [payload]
    for d in range(1, pairs):
        low = d & -d
        by_distance.append(swap(by_distance[d - low], "ctx", 2 * low))
    planes = [by_distance[d] for d in order]
    near, rows, results, got, far_got, parts = [], [], [], [], [], []

    def sides(k):
        return (("ctx", 1), ("exp", 2)) if k < count - 2 else (("exp", 2), ("ctx", 1))

    def in_steps(k):
        return k < count - 1

    def bring(k):
        if k < min(count, 3):
            one, two = sides(k)
            near.append((swap(planes[k], *one), swap(planes[k], *two), across(planes[k])))

    def bring_first(k):
        if 3 <= k < count:
            near.append((swap(planes[k], *sides(k)[0]),))

    def bring_second(k):
        if 3 <= k < count:
            near[k] = (*near[k], swap(pack((planes[k], *near[k])), *sides(k)[1]))

    def ready(k):
        own = pack((planes[k], *near[k]))
        rows.append((own, swap(own, "exp", 1)))

    def core(k):
        if 0 <= k < count:
            got.append(swap(results[k][1], "exp", 1))

    def spread(k):
        if 0 <= k < count:
            own = results[k][0]
            if in_steps(k):
                half = own.shape[0] // 2
                far_got.append((swap(summed(own, got[k], half, half).astype(BF), *sides(k)[1]),))
            else:
                last, far_got[1:] = plane_sums(own, got[k], far_got[1:])
                far_got.append(last)

    def spread_second(k):
        if 0 <= k < count and len(far_got[k]) == 1:
            first = far_got[k][0]
            size = first.shape[0] // 2
            second = summed(results[k][0], got[k], size, size) + first[size:].astype(F32)
            far_got[k] = (first, swap(second.astype(BF), *sides(k)[0]))

    def back(k):
        if 0 <= k < count:
            part = summed(results[k][0], got[k], 0, quarter)
            for v in far_got[k]:
                part = part + v[:quarter].astype(F32)
            d = order[k]
            parts.append(part if d == 0 else swap(part.astype(BF), "ctx", 2 * d))

    def sums(stage):
        core(stage - 1)
        if stage - 2 < count - 2:
            spread(stage - 2)
        spread_second(stage - 3)
        if stage == count - 1:
            spread(count - 2)
        if stage == count:
            spread_second(count - 2)
            spread(count - 1)
        back(stage - 4)

    bring(0)
    near[0], planes[1] = together(near[0], planes[1])
    for i in range(count):
        ready(i)
        sums(i)
        bring(i + 1)
        bring_second(i + 1)
        if i > 0:
            bring_first(i + 2)
        beside = (got[-1:], far_got[: count - 2], parts[-1:], near[i + 1 :], planes[i + 2 :])
        results.append(experts(*rows[i], w_gate[0], w_up[0], w_down[0], pick))
        results[i], beside = together(results[i], beside)
        got[-1:], far_got[: count - 2], parts[-1:], near[i + 1 :], planes[i + 2 :] = beside
    for i in range(count, count + 4):
        sums(i)
    for part in parts:
        hidden = hidden + part.astype(F32)
    return hidden.astype(BF)


def solution(mesh):
    in_specs = (
        P("ctx", "exp"),
        P("ctx", "exp"),
        P("ctx", None),
        P("ctx", None),
        P("exp", "ctx"),
        P("exp", "ctx"),
        P("exp"),
        P("exp", None, None),
        P("exp"),
        P("exp", "ctx"),
        P("ctx", None),
        P(),
        P("ctx", None, "exp"),
        P("ctx", None, "exp"),
        P("ctx", "exp", None),
        P("ctx", None),
        P("ctx", None),
    )
    out_specs = P(("ctx", "exp"), None)
    return jax.shard_map(local, mesh=mesh, in_specs=in_specs, out_specs=out_specs, check_vma=False)
```

```python
import jax
import jax.numpy as jnp
from jax import lax
from jax.experimental import pallas as pl
from jax.experimental.pallas import tpu as pltpu
from jax.sharding import PartitionSpec as P

PAIR = 2
eps_norm = 1e-05
BF = jnp.bfloat16
F32 = jnp.float32
LANES = 128
DOWN_TILE = 1024
GU_SLOTS = 4
DN_SLOTS = 3


def swap(x, axis, flip):
    size = lax.axis_size(axis)
    return lax.ppermute(x, axis, [(i, i ^ flip) for i in range(size)])


def mm(a, b):
    return jnp.dot(a, b, preferred_element_type=F32)


def split_total(total):
    high = total.astype(BF)
    low = (total - high.astype(F32)).astype(BF)
    both = jnp.concatenate([high, low])
    return jnp.broadcast_to(both[:, None], (both.shape[0], 128))


def with_total(state, total):
    return jnp.concatenate([state.astype(BF), split_total(total)], axis=0)


def apart(packed, heads):
    rows = packed.shape[0] - 2 * heads
    tail = packed[rows:, 0].astype(F32)
    return packed[:rows].astype(F32), tail[:heads] + tail[heads:]


def incoming_state(state, total, start, head_dim, later_use):
    place = lax.axis_index("ctx")
    pairs = lax.axis_size("ctx") // 2
    odd = place % 2 == 1
    z = place // 2
    heads = total.shape[0]
    half = heads // 2
    cut = half * head_dim
    keep = jnp.where(odd, state[cut:], state[:cut])
    keep_total = jnp.where(odd, total[half:], total[:half])
    give = jnp.where(odd, state[:cut], state[cut:])
    give_total = jnp.where(odd, total[:half], total[half:])
    got, got_total = apart(swap(with_total(give, give_total), "ctx", 1), half)

    def spread(v):
        return jnp.repeat(v, head_dim)[:, None]

    first = jnp.where(odd, got, keep)
    first_total = jnp.where(odd, got_total, keep_total)
    second = jnp.where(odd, keep, got)
    second_total = jnp.where(odd, keep_total, got_total)
    pair_state = spread(jnp.exp(-second_total)) * first + second
    pair_total = first_total + second_total
    packed = with_total(pair_state, pair_total)
    others = [apart(swap(packed, "ctx", 2 * d), half) for d in range(1, pairs)]
    states = [o[0] for o in others]
    totals = jnp.stack([o[1] for o in others])
    planes = jnp.stack([z ^ d for d in range(1, pairs)])
    between = (planes[None, :] > planes[:, None]) & (planes[None, :] < z)
    gap = jnp.sum(jnp.where(between[:, :, None], totals[None], 0.0), axis=1)
    weight = jnp.where((planes < z)[:, None], jnp.exp(-gap), 0.0)
    before = jnp.sum(jnp.where((planes < z)[:, None], totals, 0.0), axis=0)
    states, later_use = lax.optimization_barrier((states, later_use))
    own_start = jnp.where(odd, start[cut:], start[:cut])
    prefix = spread(jnp.exp(-before)) * own_start
    for i, s in enumerate(states):
        prefix = prefix + spread(weight[i]) * s
    later = spread(jnp.exp(-first_total)) * prefix + first
    mine = jnp.where(odd, later, prefix).astype(BF)
    other = swap(jnp.where(odd, prefix, later).astype(BF), "ctx", 1)
    return jnp.where(odd, other, mine), jnp.where(odd, mine, other), later_use


def mixer_rows(
    inputs, gate_input, b_proj, c_proj, step_size, decay_rate, skip_gain, start_state, later_use
):
    tok = inputs.shape[0]
    heads = step_size.shape[0]
    width = inputs.shape[1]
    head_dim = width // heads
    cumulative = jnp.cumsum(decay_rate, axis=1)
    total = cumulative[:, -1]

    def wide(v):
        return jnp.broadcast_to(v.T[:, :, None], (tok, heads, head_dim)).reshape(tok, width)

    x_local = inputs.astype(F32)
    ending = jnp.exp(-(total[:, None] - cumulative)) * step_size
    decayed = (x_local * wide(ending)).astype(BF)
    state = lax.dot_general(decayed, b_proj, (((0,), (0,)), ((), ())), preferred_element_type=F32)
    low, high, later_use = incoming_state(
        state, total, start_state.reshape(width, -1), head_dim, later_use
    )
    order = jnp.arange(tok, dtype=jnp.int32)
    causal = order[:, None] >= order[None, :]
    spread = jnp.where(causal[None], cumulative[:, :, None] - cumulative[:, None, :], 0.0)
    scores = lax.dot_general(c_proj, b_proj, (((1,), (1,)), ((), ())), preferred_element_type=F32)
    mixing = jnp.where(causal[None], jnp.exp(-spread), 0.0) * scores[None] * step_size[:, None, :]
    inside = jnp.einsum(
        "hts,shp->thp",
        mixing.astype(BF),
        inputs.reshape(tok, heads, head_dim),
        preferred_element_type=F32,
    ).reshape(tok, width)
    direct = inside + jnp.repeat(skip_gain, head_dim)[None, :] * x_local
    side = (((1,), (1,)), ((), ()))
    carried = jnp.concatenate(
        [
            lax.dot_general(c_proj, low, side, preferred_element_type=F32),
            lax.dot_general(c_proj, high, side, preferred_element_type=F32),
        ],
        axis=1,
    )
    ssm_out = direct + carried * wide(jnp.exp(-cumulative))
    return ssm_out * jax.nn.silu(gate_input.astype(F32)), later_use


def project_rows(gated, norm_gain, out_proj, neighbour_proj):
    n_exp = lax.axis_size("exp")
    n_ctx = lax.axis_size("ctx")
    me_exp = lax.axis_index("exp")
    me_ctx = lax.axis_index("ctx")
    tok, width = gated.shape
    quarter = tok // n_exp
    both = jnp.concatenate([out_proj, neighbour_proj], axis=1)
    squares = jnp.sum(gated * gated, axis=1)
    rows = (gated * norm_gain[None, :]).astype(BF)
    rel = [0, 2, 1, 3]
    pieces = [lax.dynamic_slice_in_dim(rows, (me_exp ^ q) * quarter, quarter, 0) for q in rel]
    own_rows = jnp.concatenate(pieces)
    group = [h + y for h in range(0, n_ctx, 4) for y in (0, 1)]
    arrived = [own_rows] + [swap(own_rows, "ctx", r) for r in group[1:]]
    squares, arrived[1] = lax.optimization_barrier((squares, arrived[1]))
    for flip in (1, 2):
        squares = squares + swap(squares, "exp", flip)
    own_squares = lax.dynamic_slice_in_dim(squares, me_exp * quarter, quarter, 0)
    scale = lax.rsqrt(own_squares / (width * n_exp) + eps_norm)
    full = jnp.stack(arrived).reshape(len(group), n_exp, quarter, width)
    full = full.swapaxes(0, 1).reshape(-1, width)
    partial = mm(full, both).astype(BF)
    for flip in (1, 2):
        cut = partial.shape[0] // 2
        got = swap(partial[cut:], "exp", flip)
        partial = (partial[:cut].astype(F32) + got.astype(F32)).astype(BF)
    partial, scale = lax.optimization_barrier((partial, scale))
    partial = partial.reshape(len(group), quarter, -1)
    columns = out_proj.shape[1]
    blocks = [None] * n_ctx
    for i, r in enumerate(group):
        block = partial[i] if r == 0 else swap(partial[i], "ctx", r)
        blocks[r] = block[:, :columns]
        blocks[r ^ 2] = block[:, columns:]
    stacked = jnp.stack(blocks)
    mixed = jnp.concatenate(
        [lax.dynamic_index_in_dim(stacked, me_ctx ^ b, 0, False) for b in range(n_ctx)], axis=1
    )
    return mixed.astype(F32), scale


def pack_kernel(*refs):
    out = refs[-1]
    row = 0
    for piece in refs[:-1]:
        rows = piece.shape[0]
        out[row : row + rows, :] = piece[...]
        row += rows


def pack(pieces):
    rows = sum(p.shape[0] for p in pieces)
    width = pieces[0].shape[1]
    whole = pl.BlockSpec(memory_space=pltpu.VMEM)
    return pl.pallas_call(
        pack_kernel,
        out_shape=jax.ShapeDtypeStruct((rows, width), pieces[0].dtype),
        in_specs=[whole] * len(pieces),
        out_specs=whole,
        compiler_params=pltpu.CompilerParams(vmem_limit_bytes=32 * 1024 * 1024),
        cost_estimate=pl.CostEstimate(flops=0, bytes_accessed=4 * rows * width, transcendentals=0),
    )(*pieces)


def expert_kernel(
    own, mate, gate, up, down, pick, out_own, out_mate, rows, hidden, gu, dn, row_sem, gu_sem, dn_sem
):
    half = own.shape[0]
    model = gate.shape[0]
    tiles = gate.shape[1] // LANES
    down_tiles = model // DOWN_TILE
    row_copies = [
        pltpu.make_async_copy(own, rows.at[pl.ds(0, half)], row_sem.at[0]),
        pltpu.make_async_copy(mate, rows.at[pl.ds(half, half)], row_sem.at[1]),
    ]

    def gu_copies(j):
        at = pl.ds(pl.multiple_of(j * LANES, LANES), LANES)
        s = lax.rem(j, GU_SLOTS)
        return [
            pltpu.make_async_copy(gate.at[:, at], gu.at[s, :, pl.ds(0, LANES)], gu_sem.at[s, 0]),
            pltpu.make_async_copy(up.at[:, at], gu.at[s, :, pl.ds(LANES, LANES)], gu_sem.at[s, 1]),
        ]

    def dn_copy(j):
        at = pl.ds(pl.multiple_of(j * DOWN_TILE, DOWN_TILE), DOWN_TILE)
        s = lax.rem(j, DN_SLOTS)
        return pltpu.make_async_copy(down.at[:, at], dn.at[s], dn_sem.at[s])

    for c in row_copies:
        c.start()
    for j in range(GU_SLOTS - 1):
        for c in gu_copies(j):
            c.start()
    for c in row_copies:
        c.wait()

    def gate_up(j, carry):
        ahead = j + GU_SLOTS - 1
        for c in gu_copies(j):
            c.wait()

        @pl.when(ahead < tiles)
        def _():
            for c in gu_copies(ahead):
                c.start()

        @pl.when((ahead >= tiles) & (ahead - tiles < DN_SLOTS - 1))
        def _():
            dn_copy(ahead - tiles).start()

        both = mm(rows[:, :model], gu[lax.rem(j, GU_SLOTS)])
        gate_val = both[:, :LANES]
        act = gate_val / (1.0 + jnp.exp(-gate_val)) * both[:, LANES:]
        hidden[:, pl.ds(pl.multiple_of(j * LANES, LANES), LANES)] = act.astype(BF)
        return carry

    lax.fori_loop(0, tiles, gate_up, 0)
    weight = jnp.sum(rows[:, model:].astype(F32) * pick[...], axis=1, keepdims=True)

    def down_part(j, carry):
        dn_copy(j).wait()

        @pl.when(j + DN_SLOTS - 1 < down_tiles)
        def _():
            dn_copy(j + DN_SLOTS - 1).start()

        part = mm(hidden[...], dn[lax.rem(j, DN_SLOTS)]) * weight
        at = pl.ds(pl.multiple_of(j * DOWN_TILE, DOWN_TILE), DOWN_TILE)
        out_own[:, at] = part[:half].astype(BF)
        out_mate[:, at] = part[half:].astype(BF)
        return carry

    lax.fori_loop(0, down_tiles, down_part, 0)


def experts(own, mate, gate, up, down, pick):
    half, width = own.shape
    model, units = gate.shape
    out = jax.ShapeDtypeStruct((half, model), BF)
    whole = pl.BlockSpec(memory_space=pltpu.VMEM)
    anywhere = pl.BlockSpec(memory_space=pl.ANY)
    hbm = pl.BlockSpec(memory_space=pltpu.HBM)
    flops = 2 * 2 * half * model * units * 3
    moved = 2 * (3 * model * units + 8 * half * model)
    return pl.pallas_call(
        expert_kernel,
        out_shape=(out, out),
        in_specs=[anywhere] * 2 + [hbm] * 3 + [whole],
        out_specs=(whole, whole),
        scratch_shapes=[
            pltpu.VMEM((2 * half, width), BF),
            pltpu.VMEM((2 * half, units), BF),
            pltpu.VMEM((GU_SLOTS, model, 2 * LANES), BF),
            pltpu.VMEM((DN_SLOTS, units, DOWN_TILE), BF),
            pltpu.SemaphoreType.DMA((2,)),
            pltpu.SemaphoreType.DMA((GU_SLOTS, 2)),
            pltpu.SemaphoreType.DMA((DN_SLOTS,)),
        ],
        compiler_params=pltpu.CompilerParams(vmem_limit_bytes=48 * 1024 * 1024),
        cost_estimate=pl.CostEstimate(flops=flops, bytes_accessed=moved, transcendentals=2 * half * units),
    )(own, mate, gate, up, down, pick)


def together(values, others):
    return lax.optimization_barrier((tuple(values), others))


def across(x):
    n_ctx, n_exp = lax.axis_size("ctx"), lax.axis_size("exp")
    pairs = [
        (c * n_exp + e, (c ^ 1) * n_exp + (e ^ 2)) for c in range(n_ctx) for e in range(n_exp)
    ]
    return lax.ppermute(x, ("ctx", "exp"), pairs)


def summed(own, got, first, rows):
    last = first + rows
    return own[first:last].astype(F32) + got[first:last].astype(F32)


def plane_sums(own, got, others):
    size = own.shape[0] // 4
    sums = [summed(own, got, k * size, size).astype(BF) for k in (1, 2, 3)]
    (to_x,), others = together(sums[:1], others)
    return (swap(to_x, "exp", 2), swap(sums[1], "ctx", 1), across(sums[2])), others


def local(
    inputs,
    gate_input,
    b_proj,
    c_proj,
    step_size,
    decay_rate,
    skip_gain,
    start_state,
    norm_gain,
    out_proj,
    residual,
    moe_gain,
    w_gate,
    w_up,
    w_down,
    route_ids,
    route_gates,
):
    n_ctx = lax.axis_size("ctx")
    n_exp = lax.axis_size("exp")
    me_ctx = lax.axis_index("ctx")
    me_exp = lax.axis_index("exp")
    tok = inputs.shape[0]
    quarter = tok // n_exp
    pairs = n_ctx // 2
    named = route_ids[:, :, None] == jnp.arange(LANES // 2, dtype=jnp.int32)[None, None, :]
    weights = jnp.sum(jnp.where(named, route_gates[:, :, None], 0.0), axis=1)
    weights = lax.dynamic_slice_in_dim(weights, me_exp * quarter, quarter, 0)
    weights_high = weights.astype(BF)
    weights_low = (weights - weights_high.astype(F32)).astype(BF)
    lane = jnp.arange(LANES, dtype=jnp.int32)
    pick = (lane % (LANES // 2) == me_ctx // PAIR).astype(F32)[None, :]

    cut = out_proj.shape[0] // 4
    two_parts = (swap(out_proj[:cut], "ctx", 2), out_proj[cut:])
    gated, (first_part, second_part) = mixer_rows(
        inputs, gate_input, b_proj, c_proj, step_size, decay_rate, skip_gain, start_state, two_parts
    )
    neighbour_proj = jnp.concatenate([first_part, swap(second_part, "ctx", 2)])
    mixed, scale = project_rows(gated, norm_gain, out_proj, neighbour_proj)
    own_residual = lax.dynamic_slice_in_dim(residual, me_exp * quarter, quarter, 0)
    hidden = own_residual.astype(F32) + mixed * scale[:, None]
    moe_scale = lax.rsqrt(jnp.mean(hidden * hidden, axis=1, keepdims=True) + eps_norm)
    moe_in = (hidden * moe_scale * moe_gain[None, :]).astype(BF)

    payload = jnp.concatenate([moe_in, weights_high, weights_low], axis=1)
    order = [0] + list(range(2, pairs)) + [1]
    count = len(order)
    by_distance = [payload]
    for d in range(1, pairs):
        low = d & -d
        by_distance.append(swap(by_distance[d - low], "ctx", 2 * low))
    planes = [by_distance[d] for d in order]
    near, rows, results, got, far_got, parts = [], [], [], [], [], []

    def sides(k):
        return (("ctx", 1), ("exp", 2)) if k < count - 2 else (("exp", 2), ("ctx", 1))

    def in_steps(k):
        return k < count - 1

    def bring(k):
        if k < min(count, 3):
            one, two = sides(k)
            near.append((swap(planes[k], *one), swap(planes[k], *two), across(planes[k])))

    def bring_first(k):
        if 3 <= k < count:
            near.append((swap(planes[k], *sides(k)[0]),))

    def bring_second(k):
        if 3 <= k < count:
            near[k] = (*near[k], swap(pack((planes[k], *near[k])), *sides(k)[1]))

    def ready(k):
        own = pack((planes[k], *near[k]))
        rows.append((own, swap(own, "exp", 1)))

    def core(k):
        if 0 <= k < count:
            got.append(swap(results[k][1], "exp", 1))

    def spread(k):
        if 0 <= k < count:
            own = results[k][0]
            if in_steps(k):
                half = own.shape[0] // 2
                far_got.append((swap(summed(own, got[k], half, half).astype(BF), *sides(k)[1]),))
            else:
                last, far_got[1:] = plane_sums(own, got[k], far_got[1:])
                far_got.append(last)

    def spread_second(k):
        if 0 <= k < count and len(far_got[k]) == 1:
            first = far_got[k][0]
            size = first.shape[0] // 2
            second = summed(results[k][0], got[k], size, size) + first[size:].astype(F32)
            far_got[k] = (first, swap(second.astype(BF), *sides(k)[0]))

    def back(k):
        if 0 <= k < count:
            part = summed(results[k][0], got[k], 0, quarter)
            for v in far_got[k]:
                part = part + v[:quarter].astype(F32)
            d = order[k]
            parts.append(part if d == 0 else swap(part.astype(BF), "ctx", 2 * d))

    def sums(stage):
        core(stage - 1)
        if stage - 2 < count - 2:
            spread(stage - 2)
        spread_second(stage - 3)
        if stage == count - 1:
            spread(count - 2)
        if stage == count:
            spread_second(count - 2)
            spread(count - 1)
        back(stage - 4)

    bring(0)
    near[0], planes[1] = together(near[0], planes[1])
    for i in range(count):
        ready(i)
        sums(i)
        bring(i + 1)
        bring_second(i + 1)
        if i > 0:
            bring_first(i + 2)
        beside = (got[-1:], far_got[: count - 2], parts[-1:], near[i + 1 : i + 2], planes[i + 2 :])
        results.append(experts(*rows[i], w_gate[0], w_up[0], w_down[0], pick))
        results[i], beside = together(results[i], beside)
        got[-1:], far_got[: count - 2], parts[-1:], near[i + 1 : i + 2], planes[i + 2 :] = beside
    for i in range(count, count + 4):
        sums(i)
    for part in parts:
        hidden = hidden + part.astype(F32)
    return hidden.astype(BF)


def solution(mesh):
    in_specs = (
        P("ctx", "exp"),
        P("ctx", "exp"),
        P("ctx", None),
        P("ctx", None),
        P("exp", "ctx"),
        P("exp", "ctx"),
        P("exp"),
        P("exp", None, None),
        P("exp"),
        P("exp", "ctx"),
        P("ctx", None),
        P(),
        P("ctx", None, "exp"),
        P("ctx", None, "exp"),
        P("ctx", "exp", None),
        P("ctx", None),
        P("ctx", None),
    )
    out_specs = P(("ctx", "exp"), None)
    return jax.shard_map(local, mesh=mesh, in_specs=in_specs, out_specs=out_specs, check_vma=False)
```

```python
import jax
import jax.numpy as jnp
from jax import lax
from jax.experimental import pallas as pl
from jax.experimental.pallas import tpu as pltpu
from jax.sharding import PartitionSpec as P

PAIR = 2
eps_norm = 1e-05
BF = jnp.bfloat16
F32 = jnp.float32
LANES = 128
DOWN_TILE = 1024
GU_SLOTS = 4
DN_SLOTS = 3


def swap(x, axis, flip):
    size = lax.axis_size(axis)
    return lax.ppermute(x, axis, [(i, i ^ flip) for i in range(size)])


def mm(a, b):
    return jnp.dot(a, b, preferred_element_type=F32)


def split_total(total):
    high = total.astype(BF)
    low = (total - high.astype(F32)).astype(BF)
    both = jnp.concatenate([high, low])
    return jnp.broadcast_to(both[:, None], (both.shape[0], 128))


def with_total(state, total):
    return jnp.concatenate([state.astype(BF), split_total(total)], axis=0)


def apart(packed, heads):
    rows = packed.shape[0] - 2 * heads
    tail = packed[rows:, 0].astype(F32)
    return packed[:rows].astype(F32), tail[:heads] + tail[heads:]


def prefix_kernel(where, start, first, first_total, *refs):
    arrived, (mine, other) = refs[:-2], refs[-2:]
    z, odd = where[0], where[1] == 1
    rows, lanes = first.shape
    heads = first_total.shape[0]

    def by_head(values):
        return values.reshape(heads, rows // heads, lanes)

    totals = [
        a[rows : rows + heads, :].astype(F32) + a[rows + heads : rows + 2 * heads, :].astype(F32)
        for a in arrived
    ]
    planes = [z ^ d for d in range(1, len(arrived) + 1)]
    before = jnp.zeros_like(totals[0])
    weights = []
    for i in range(len(arrived)):
        gap = jnp.zeros_like(before)
        for j in range(len(arrived)):
            if j != i:
                between = (planes[j] > planes[i]) & (planes[j] < z)
                gap = gap + jnp.where(between, totals[j], 0.0)
        weights.append(jnp.where(planes[i] < z, jnp.exp(-gap), 0.0))
        before = before + jnp.where(planes[i] < z, totals[i], 0.0)
    own_start = jnp.where(odd, start[rows:, :], start[:rows, :])
    prefix = jnp.exp(-before)[:, None, :] * by_head(own_start)
    for weight, a in zip(weights, arrived):
        prefix = prefix + weight[:, None, :] * by_head(a[:rows, :].astype(F32))
    later = jnp.exp(-first_total[...])[:, None, :] * prefix + by_head(first[...])
    mine[...] = jnp.where(odd, later, prefix).reshape(rows, lanes).astype(BF)
    other[...] = jnp.where(odd, prefix, later).reshape(rows, lanes).astype(BF)


def prefix_states(where, start, first, first_total, arrived):
    out = jax.ShapeDtypeStruct(first.shape, BF)
    whole = pl.BlockSpec(memory_space=pltpu.VMEM)
    return pl.pallas_call(
        prefix_kernel,
        out_shape=(out, out),
        in_specs=[pl.BlockSpec(memory_space=pltpu.SMEM)] + [whole] * (3 + len(arrived)),
        out_specs=(whole, whole),
        compiler_params=pltpu.CompilerParams(vmem_limit_bytes=16 * 1024 * 1024),
    )(where, start, first, first_total, *arrived)


def incoming_state(state, total, start, head_dim, later_use):
    place = lax.axis_index("ctx")
    pairs = lax.axis_size("ctx") // 2
    odd = place % 2 == 1
    z = place // 2
    heads = total.shape[0]
    half = heads // 2
    cut = half * head_dim
    keep = jnp.where(odd, state[cut:], state[:cut])
    keep_total = jnp.where(odd, total[half:], total[:half])
    give = jnp.where(odd, state[:cut], state[cut:])
    give_total = jnp.where(odd, total[:half], total[half:])
    got, got_total = apart(swap(with_total(give, give_total), "ctx", 1), half)

    def spread(v):
        return jnp.repeat(v, head_dim)[:, None]

    first = jnp.where(odd, got, keep)
    first_total = jnp.where(odd, got_total, keep_total)
    second = jnp.where(odd, keep, got)
    second_total = jnp.where(odd, keep_total, got_total)
    pair_state = spread(jnp.exp(-second_total)) * first + second
    pair_total = first_total + second_total
    packed = with_total(pair_state, pair_total)
    arrived = [swap(packed, "ctx", 2 * d) for d in range(1, pairs)]
    arrived, later_use = lax.optimization_barrier((arrived, later_use))
    where = jnp.stack([z, place % 2]).astype(jnp.int32)
    lanes = state.shape[1]
    first_wide = jnp.broadcast_to(first_total[:, None], (half, lanes))
    mine, sent = prefix_states(where, start, first, first_wide, arrived)
    other = swap(sent, "ctx", 1)
    return jnp.where(odd, other, mine), jnp.where(odd, mine, other), later_use


def mixer_rows(
    inputs, gate_input, b_proj, c_proj, step_size, decay_rate, skip_gain, start_state, later_use
):
    tok = inputs.shape[0]
    heads = step_size.shape[0]
    width = inputs.shape[1]
    head_dim = width // heads
    cumulative = jnp.cumsum(decay_rate, axis=1)
    total = cumulative[:, -1]

    def wide(v):
        return jnp.broadcast_to(v.T[:, :, None], (tok, heads, head_dim)).reshape(tok, width)

    x_local = inputs.astype(F32)
    ending = jnp.exp(-(total[:, None] - cumulative)) * step_size
    decayed = (x_local * wide(ending)).astype(BF)
    state = lax.dot_general(decayed, b_proj, (((0,), (0,)), ((), ())), preferred_element_type=F32)
    low, high, later_use = incoming_state(
        state, total, start_state.reshape(width, -1), head_dim, later_use
    )
    order = jnp.arange(tok, dtype=jnp.int32)
    causal = order[:, None] >= order[None, :]
    spread = jnp.where(causal[None], cumulative[:, :, None] - cumulative[:, None, :], 0.0)
    scores = lax.dot_general(c_proj, b_proj, (((1,), (1,)), ((), ())), preferred_element_type=F32)
    mixing = jnp.where(causal[None], jnp.exp(-spread), 0.0) * scores[None] * step_size[:, None, :]
    inside = jnp.einsum(
        "hts,shp->thp",
        mixing.astype(BF),
        inputs.reshape(tok, heads, head_dim),
        preferred_element_type=F32,
    ).reshape(tok, width)
    direct = inside + jnp.repeat(skip_gain, head_dim)[None, :] * x_local
    side = (((1,), (1,)), ((), ()))
    carried = jnp.concatenate(
        [
            lax.dot_general(c_proj, low, side, preferred_element_type=F32),
            lax.dot_general(c_proj, high, side, preferred_element_type=F32),
        ],
        axis=1,
    )
    ssm_out = direct + carried * wide(jnp.exp(-cumulative))
    return ssm_out * jax.nn.silu(gate_input.astype(F32)), later_use


def project_rows(gated, norm_gain, out_proj, neighbour_proj):
    n_exp = lax.axis_size("exp")
    n_ctx = lax.axis_size("ctx")
    me_exp = lax.axis_index("exp")
    me_ctx = lax.axis_index("ctx")
    tok, width = gated.shape
    quarter = tok // n_exp
    both = jnp.concatenate([out_proj, neighbour_proj], axis=1)
    squares = jnp.sum(gated * gated, axis=1)
    rows = (gated * norm_gain[None, :]).astype(BF)
    rel = [0, 2, 1, 3]
    pieces = [lax.dynamic_slice_in_dim(rows, (me_exp ^ q) * quarter, quarter, 0) for q in rel]
    own_rows = jnp.concatenate(pieces)
    group = [h + y for h in range(0, n_ctx, 4) for y in (0, 1)]
    arrived = [own_rows] + [swap(own_rows, "ctx", r) for r in group[1:]]
    squares, arrived[1] = lax.optimization_barrier((squares, arrived[1]))
    for flip in (1, 2):
        squares = squares + swap(squares, "exp", flip)
    own_squares = lax.dynamic_slice_in_dim(squares, me_exp * quarter, quarter, 0)
    scale = lax.rsqrt(own_squares / (width * n_exp) + eps_norm)
    full = jnp.stack(arrived).reshape(len(group), n_exp, quarter, width)
    full = full.swapaxes(0, 1).reshape(-1, width)
    partial = mm(full, both).astype(BF)
    for flip in (1, 2):
        cut = partial.shape[0] // 2
        got = swap(partial[cut:], "exp", flip)
        partial = (partial[:cut].astype(F32) + got.astype(F32)).astype(BF)
    partial, scale = lax.optimization_barrier((partial, scale))
    partial = partial.reshape(len(group), quarter, -1)
    columns = out_proj.shape[1]
    blocks = [None] * n_ctx
    for i, r in enumerate(group):
        block = partial[i] if r == 0 else swap(partial[i], "ctx", r)
        blocks[r] = block[:, :columns]
        blocks[r ^ 2] = block[:, columns:]
    stacked = jnp.stack(blocks)
    mixed = jnp.concatenate(
        [lax.dynamic_index_in_dim(stacked, me_ctx ^ b, 0, False) for b in range(n_ctx)], axis=1
    )
    return mixed.astype(F32), scale


def pack_kernel(*refs):
    out = refs[-1]
    row = 0
    for piece in refs[:-1]:
        rows = piece.shape[0]
        out[row : row + rows, :] = piece[...]
        row += rows


def pack(pieces):
    rows = sum(p.shape[0] for p in pieces)
    width = pieces[0].shape[1]
    whole = pl.BlockSpec(memory_space=pltpu.VMEM)
    return pl.pallas_call(
        pack_kernel,
        out_shape=jax.ShapeDtypeStruct((rows, width), pieces[0].dtype),
        in_specs=[whole] * len(pieces),
        out_specs=whole,
        compiler_params=pltpu.CompilerParams(vmem_limit_bytes=32 * 1024 * 1024),
        cost_estimate=pl.CostEstimate(flops=0, bytes_accessed=4 * rows * width, transcendentals=0),
    )(*pieces)


def expert_kernel(
    own, mate, gate, up, down, pick, out_own, out_mate, rows, hidden, gu, dn, row_sem, gu_sem, dn_sem
):
    half = own.shape[0]
    model = gate.shape[0]
    tiles = gate.shape[1] // LANES
    down_tiles = model // DOWN_TILE
    row_copies = [
        pltpu.make_async_copy(own, rows.at[pl.ds(0, half)], row_sem.at[0]),
        pltpu.make_async_copy(mate, rows.at[pl.ds(half, half)], row_sem.at[1]),
    ]

    def gu_copies(j):
        at = pl.ds(pl.multiple_of(j * LANES, LANES), LANES)
        s = lax.rem(j, GU_SLOTS)
        return [
            pltpu.make_async_copy(gate.at[:, at], gu.at[s, :, pl.ds(0, LANES)], gu_sem.at[s, 0]),
            pltpu.make_async_copy(up.at[:, at], gu.at[s, :, pl.ds(LANES, LANES)], gu_sem.at[s, 1]),
        ]

    def dn_copy(j):
        at = pl.ds(pl.multiple_of(j * DOWN_TILE, DOWN_TILE), DOWN_TILE)
        s = lax.rem(j, DN_SLOTS)
        return pltpu.make_async_copy(down.at[:, at], dn.at[s], dn_sem.at[s])

    for c in row_copies:
        c.start()
    for j in range(GU_SLOTS - 1):
        for c in gu_copies(j):
            c.start()
    for c in row_copies:
        c.wait()

    def gate_up(j, carry):
        ahead = j + GU_SLOTS - 1
        for c in gu_copies(j):
            c.wait()

        @pl.when(ahead < tiles)
        def _():
            for c in gu_copies(ahead):
                c.start()

        @pl.when((ahead >= tiles) & (ahead - tiles < DN_SLOTS - 1))
        def _():
            dn_copy(ahead - tiles).start()

        both = mm(rows[:, :model], gu[lax.rem(j, GU_SLOTS)])
        gate_val = both[:, :LANES]
        act = gate_val / (1.0 + jnp.exp(-gate_val)) * both[:, LANES:]
        hidden[:, pl.ds(pl.multiple_of(j * LANES, LANES), LANES)] = act.astype(BF)
        return carry

    lax.fori_loop(0, tiles, gate_up, 0)
    weight = jnp.sum(rows[:, model:].astype(F32) * pick[...], axis=1, keepdims=True)

    def down_part(j, carry):
        dn_copy(j).wait()

        @pl.when(j + DN_SLOTS - 1 < down_tiles)
        def _():
            dn_copy(j + DN_SLOTS - 1).start()

        part = mm(hidden[...], dn[lax.rem(j, DN_SLOTS)]) * weight
        at = pl.ds(pl.multiple_of(j * DOWN_TILE, DOWN_TILE), DOWN_TILE)
        out_own[:, at] = part[:half].astype(BF)
        out_mate[:, at] = part[half:].astype(BF)
        return carry

    lax.fori_loop(0, down_tiles, down_part, 0)


def experts(own, mate, gate, up, down, pick):
    half, width = own.shape
    model, units = gate.shape
    out = jax.ShapeDtypeStruct((half, model), BF)
    whole = pl.BlockSpec(memory_space=pltpu.VMEM)
    anywhere = pl.BlockSpec(memory_space=pl.ANY)
    hbm = pl.BlockSpec(memory_space=pltpu.HBM)
    flops = 2 * 2 * half * model * units * 3
    moved = 2 * (3 * model * units + 8 * half * model)
    return pl.pallas_call(
        expert_kernel,
        out_shape=(out, out),
        in_specs=[anywhere] * 2 + [hbm] * 3 + [whole],
        out_specs=(whole, whole),
        scratch_shapes=[
            pltpu.VMEM((2 * half, width), BF),
            pltpu.VMEM((2 * half, units), BF),
            pltpu.VMEM((GU_SLOTS, model, 2 * LANES), BF),
            pltpu.VMEM((DN_SLOTS, units, DOWN_TILE), BF),
            pltpu.SemaphoreType.DMA((2,)),
            pltpu.SemaphoreType.DMA((GU_SLOTS, 2)),
            pltpu.SemaphoreType.DMA((DN_SLOTS,)),
        ],
        compiler_params=pltpu.CompilerParams(vmem_limit_bytes=48 * 1024 * 1024),
        cost_estimate=pl.CostEstimate(flops=flops, bytes_accessed=moved, transcendentals=2 * half * units),
    )(own, mate, gate, up, down, pick)


def together(values, others):
    return lax.optimization_barrier((tuple(values), others))


def across(x):
    n_ctx, n_exp = lax.axis_size("ctx"), lax.axis_size("exp")
    pairs = [
        (c * n_exp + e, (c ^ 1) * n_exp + (e ^ 2)) for c in range(n_ctx) for e in range(n_exp)
    ]
    return lax.ppermute(x, ("ctx", "exp"), pairs)


def summed(own, got, first, rows):
    last = first + rows
    return own[first:last].astype(F32) + got[first:last].astype(F32)


def plane_sums(own, got, others):
    size = own.shape[0] // 4
    sums = [summed(own, got, k * size, size).astype(BF) for k in (1, 2, 3)]
    (to_x,), others = together(sums[:1], others)
    return (swap(to_x, "exp", 2), swap(sums[1], "ctx", 1), across(sums[2])), others


def local(
    inputs,
    gate_input,
    b_proj,
    c_proj,
    step_size,
    decay_rate,
    skip_gain,
    start_state,
    norm_gain,
    out_proj,
    residual,
    moe_gain,
    w_gate,
    w_up,
    w_down,
    route_ids,
    route_gates,
):
    n_ctx = lax.axis_size("ctx")
    n_exp = lax.axis_size("exp")
    me_ctx = lax.axis_index("ctx")
    me_exp = lax.axis_index("exp")
    tok = inputs.shape[0]
    quarter = tok // n_exp
    pairs = n_ctx // 2
    named = route_ids[:, :, None] == jnp.arange(LANES // 2, dtype=jnp.int32)[None, None, :]
    weights = jnp.sum(jnp.where(named, route_gates[:, :, None], 0.0), axis=1)
    weights = lax.dynamic_slice_in_dim(weights, me_exp * quarter, quarter, 0)
    weights_high = weights.astype(BF)
    weights_low = (weights - weights_high.astype(F32)).astype(BF)
    lane = jnp.arange(LANES, dtype=jnp.int32)
    pick = (lane % (LANES // 2) == me_ctx // PAIR).astype(F32)[None, :]

    cut = out_proj.shape[0] // 4
    two_parts = (swap(out_proj[:cut], "ctx", 2), out_proj[cut:])
    gated, (first_part, second_part) = mixer_rows(
        inputs, gate_input, b_proj, c_proj, step_size, decay_rate, skip_gain, start_state, two_parts
    )
    neighbour_proj = jnp.concatenate([first_part, swap(second_part, "ctx", 2)])
    mixed, scale = project_rows(gated, norm_gain, out_proj, neighbour_proj)
    own_residual = lax.dynamic_slice_in_dim(residual, me_exp * quarter, quarter, 0)
    hidden = own_residual.astype(F32) + mixed * scale[:, None]
    moe_scale = lax.rsqrt(jnp.mean(hidden * hidden, axis=1, keepdims=True) + eps_norm)
    moe_in = (hidden * moe_scale * moe_gain[None, :]).astype(BF)

    payload = jnp.concatenate([moe_in, weights_high, weights_low], axis=1)
    order = [0] + list(range(2, pairs)) + [1]
    count = len(order)
    by_distance = [payload]
    for d in range(1, pairs):
        low = d & -d
        by_distance.append(swap(by_distance[d - low], "ctx", 2 * low))
    planes = [by_distance[d] for d in order]
    near, rows, results, got, far_got, parts = [], [], [], [], [], []

    def sides(k):
        return (("ctx", 1), ("exp", 2)) if k < count - 2 else (("exp", 2), ("ctx", 1))

    def in_steps(k):
        return k < count - 1

    def bring(k):
        if k < min(count, 3):
            one, two = sides(k)
            near.append((swap(planes[k], *one), swap(planes[k], *two), across(planes[k])))

    def bring_first(k):
        if 3 <= k < count:
            near.append((swap(planes[k], *sides(k)[0]),))

    def bring_second(k):
        if 3 <= k < count:
            near[k] = (*near[k], swap(pack((planes[k], *near[k])), *sides(k)[1]))

    def ready(k):
        own = pack((planes[k], *near[k]))
        rows.append((own, swap(own, "exp", 1)))

    def core(k):
        if 0 <= k < count:
            got.append(swap(results[k][1], "exp", 1))

    def spread(k):
        if 0 <= k < count:
            own = results[k][0]
            if in_steps(k):
                half = own.shape[0] // 2
                far_got.append((swap(summed(own, got[k], half, half).astype(BF), *sides(k)[1]),))
            else:
                last, far_got[1:] = plane_sums(own, got[k], far_got[1:])
                far_got.append(last)

    def spread_second(k):
        if 0 <= k < count and len(far_got[k]) == 1:
            first = far_got[k][0]
            size = first.shape[0] // 2
            second = summed(results[k][0], got[k], size, size) + first[size:].astype(F32)
            far_got[k] = (first, swap(second.astype(BF), *sides(k)[0]))

    def back(k):
        if 0 <= k < count:
            part = summed(results[k][0], got[k], 0, quarter)
            for v in far_got[k]:
                part = part + v[:quarter].astype(F32)
            d = order[k]
            parts.append(part if d == 0 else swap(part.astype(BF), "ctx", 2 * d))

    def sums(stage):
        core(stage - 1)
        if stage - 2 < count - 2:
            spread(stage - 2)
        spread_second(stage - 3)
        if stage == count - 1:
            spread(count - 2)
        if stage == count:
            spread_second(count - 2)
            spread(count - 1)
        back(stage - 4)

    bring(0)
    near[0], planes[1] = together(near[0], planes[1])
    for i in range(count):
        ready(i)
        sums(i)
        bring(i + 1)
        bring_second(i + 1)
        if i > 0:
            bring_first(i + 2)
        beside = (got[-1:], far_got[: count - 2], parts[-1:], near[i + 1 : i + 2], planes[i + 2 :])
        results.append(experts(*rows[i], w_gate[0], w_up[0], w_down[0], pick))
        results[i], beside = together(results[i], beside)
        got[-1:], far_got[: count - 2], parts[-1:], near[i + 1 : i + 2], planes[i + 2 :] = beside
    for i in range(count, count + 4):
        sums(i)
    for part in parts:
        hidden = hidden + part.astype(F32)
    return hidden.astype(BF)


def solution(mesh):
    in_specs = (
        P("ctx", "exp"),
        P("ctx", "exp"),
        P("ctx", None),
        P("ctx", None),
        P("exp", "ctx"),
        P("exp", "ctx"),
        P("exp"),
        P("exp", None, None),
        P("exp"),
        P("exp", "ctx"),
        P("ctx", None),
        P(),
        P("ctx", None, "exp"),
        P("ctx", None, "exp"),
        P("ctx", "exp", None),
        P("ctx", None),
        P("ctx", None),
    )
    out_specs = P(("ctx", "exp"), None)
    return jax.shard_map(local, mesh=mesh, in_specs=in_specs, out_specs=out_specs, check_vma=False)
```

```python
import jax
import jax.numpy as jnp
from jax import lax
from jax.experimental import pallas as pl
from jax.experimental.pallas import tpu as pltpu
from jax.sharding import PartitionSpec as P

PAIR = 2
eps_norm = 1e-05
BF = jnp.bfloat16
F32 = jnp.float32
LANES = 128
DOWN_TILE = 1024
GU_SLOTS = 4
DN_SLOTS = 3


def swap(x, axis, flip):
    size = lax.axis_size(axis)
    return lax.ppermute(x, axis, [(i, i ^ flip) for i in range(size)])


def mm(a, b):
    return jnp.dot(a, b, preferred_element_type=F32)


def split_total(total):
    high = total.astype(BF)
    low = (total - high.astype(F32)).astype(BF)
    both = jnp.concatenate([high, low])
    return jnp.broadcast_to(both[:, None], (both.shape[0], 128))


def with_total(state, total):
    return jnp.concatenate([state.astype(BF), split_total(total)], axis=0)


def apart(packed, heads):
    rows = packed.shape[0] - 2 * heads
    tail = packed[rows:, 0].astype(F32)
    return packed[:rows].astype(F32), tail[:heads] + tail[heads:]


def prefix_kernel(where, start, first, first_total, *refs):
    arrived, (mine, other) = refs[:-2], refs[-2:]
    z, odd = where[0], where[1] == 1
    rows, lanes = first.shape
    heads = first_total.shape[0]

    def by_head(values):
        return values.reshape(heads, rows // heads, lanes)

    totals = [
        a[rows : rows + heads, :].astype(F32) + a[rows + heads : rows + 2 * heads, :].astype(F32)
        for a in arrived
    ]
    planes = [z ^ d for d in range(1, len(arrived) + 1)]
    before = jnp.zeros_like(totals[0])
    weights = []
    for i in range(len(arrived)):
        gap = jnp.zeros_like(before)
        for j in range(len(arrived)):
            if j != i:
                between = (planes[j] > planes[i]) & (planes[j] < z)
                gap = gap + jnp.where(between, totals[j], 0.0)
        weights.append(jnp.where(planes[i] < z, jnp.exp(-gap), 0.0))
        before = before + jnp.where(planes[i] < z, totals[i], 0.0)
    own_start = jnp.where(odd, start[rows:, :], start[:rows, :])
    prefix = jnp.exp(-before)[:, None, :] * by_head(own_start)
    for weight, a in zip(weights, arrived):
        prefix = prefix + weight[:, None, :] * by_head(a[:rows, :].astype(F32))
    later = jnp.exp(-first_total[...])[:, None, :] * prefix + by_head(first[...])
    mine[...] = jnp.where(odd, later, prefix).reshape(rows, lanes).astype(BF)
    other[...] = jnp.where(odd, prefix, later).reshape(rows, lanes).astype(BF)


def prefix_states(where, start, first, first_total, arrived):
    out = jax.ShapeDtypeStruct(first.shape, BF)
    whole = pl.BlockSpec(memory_space=pltpu.VMEM)
    return pl.pallas_call(
        prefix_kernel,
        out_shape=(out, out),
        in_specs=[pl.BlockSpec(memory_space=pltpu.SMEM)] + [whole] * (3 + len(arrived)),
        out_specs=(whole, whole),
        compiler_params=pltpu.CompilerParams(vmem_limit_bytes=16 * 1024 * 1024),
    )(where, start, first, first_total, *arrived)


def incoming_state(state, total, start, head_dim, later_use):
    place = lax.axis_index("ctx")
    pairs = lax.axis_size("ctx") // 2
    odd = place % 2 == 1
    z = place // 2
    heads = total.shape[0]
    half = heads // 2
    cut = half * head_dim
    keep = jnp.where(odd, state[cut:], state[:cut])
    keep_total = jnp.where(odd, total[half:], total[:half])
    give = jnp.where(odd, state[:cut], state[cut:])
    give_total = jnp.where(odd, total[:half], total[half:])
    got, got_total = apart(swap(with_total(give, give_total), "ctx", 1), half)

    def spread(v):
        return jnp.repeat(v, head_dim)[:, None]

    first = jnp.where(odd, got, keep)
    first_total = jnp.where(odd, got_total, keep_total)
    second = jnp.where(odd, keep, got)
    second_total = jnp.where(odd, keep_total, got_total)
    pair_state = spread(jnp.exp(-second_total)) * first + second
    pair_total = first_total + second_total
    packed = with_total(pair_state, pair_total)
    arrived = [swap(packed, "ctx", 2 * d) for d in range(1, pairs)]
    arrived, later_use = lax.optimization_barrier((arrived, later_use))
    where = jnp.stack([z, place % 2]).astype(jnp.int32)
    lanes = state.shape[1]
    first_wide = jnp.broadcast_to(first_total[:, None], (half, lanes))
    mine, sent = prefix_states(where, start, first, first_wide, arrived)
    other = swap(sent, "ctx", 1)
    return jnp.where(odd, other, mine), jnp.where(odd, mine, other), later_use


def mixer_rows(
    inputs, gate_input, b_proj, c_proj, step_size, decay_rate, skip_gain, start_state, later_use
):
    tok = inputs.shape[0]
    heads = step_size.shape[0]
    width = inputs.shape[1]
    head_dim = width // heads
    cumulative = jnp.cumsum(decay_rate, axis=1)
    total = cumulative[:, -1]

    def wide(v):
        return jnp.broadcast_to(v.T[:, :, None], (tok, heads, head_dim)).reshape(tok, width)

    x_local = inputs.astype(F32)
    ending = jnp.exp(-(total[:, None] - cumulative)) * step_size
    decayed = (x_local * wide(ending)).astype(BF)
    state = lax.dot_general(decayed, b_proj, (((0,), (0,)), ((), ())), preferred_element_type=F32)
    low, high, later_use = incoming_state(
        state, total, start_state.reshape(width, -1), head_dim, later_use
    )
    order = jnp.arange(tok, dtype=jnp.int32)
    causal = order[:, None] >= order[None, :]
    spread = jnp.where(causal[None], cumulative[:, :, None] - cumulative[:, None, :], 0.0)
    scores = lax.dot_general(c_proj, b_proj, (((1,), (1,)), ((), ())), preferred_element_type=F32)
    mixing = jnp.where(causal[None], jnp.exp(-spread), 0.0) * scores[None] * step_size[:, None, :]
    inside = jnp.einsum(
        "hts,shp->thp",
        mixing.astype(BF),
        inputs.reshape(tok, heads, head_dim),
        preferred_element_type=F32,
    ).reshape(tok, width)
    direct = inside + jnp.repeat(skip_gain, head_dim)[None, :] * x_local
    side = (((1,), (1,)), ((), ()))
    carried = jnp.concatenate(
        [
            lax.dot_general(c_proj, low, side, preferred_element_type=F32),
            lax.dot_general(c_proj, high, side, preferred_element_type=F32),
        ],
        axis=1,
    )
    ssm_out = direct + carried * wide(jnp.exp(-cumulative))
    return ssm_out * jax.nn.silu(gate_input.astype(F32)), later_use


def project_rows(gated, norm_gain, out_proj, neighbour_proj):
    n_exp = lax.axis_size("exp")
    n_ctx = lax.axis_size("ctx")
    me_exp = lax.axis_index("exp")
    me_ctx = lax.axis_index("ctx")
    tok, width = gated.shape
    quarter = tok // n_exp
    both = jnp.concatenate([out_proj, neighbour_proj], axis=1)
    squares = jnp.sum(gated * gated, axis=1)
    rows = (gated * norm_gain[None, :]).astype(BF)
    rel = [0, 2, 1, 3]
    pieces = [lax.dynamic_slice_in_dim(rows, (me_exp ^ q) * quarter, quarter, 0) for q in rel]
    own_rows = jnp.concatenate(pieces)
    group = [h + y for h in range(0, n_ctx, 4) for y in (0, 1)]
    arrived = []
    for h in range(0, n_ctx, 4):
        along_z = own_rows if h == 0 else swap(own_rows, "ctx", h)
        arrived += [along_z, swap(along_z, "ctx", 1)]
    squares, arrived[1] = lax.optimization_barrier((squares, arrived[1]))
    for flip in (1, 2):
        squares = squares + swap(squares, "exp", flip)
    own_squares = lax.dynamic_slice_in_dim(squares, me_exp * quarter, quarter, 0)
    scale = lax.rsqrt(own_squares / (width * n_exp) + eps_norm)
    full = jnp.stack(arrived).reshape(len(group), n_exp, quarter, width)
    full = full.swapaxes(0, 1).reshape(-1, width)
    partial = mm(full, both).astype(BF)
    for flip in (1, 2):
        cut = partial.shape[0] // 2
        got = swap(partial[cut:], "exp", flip)
        partial = (partial[:cut].astype(F32) + got.astype(F32)).astype(BF)
    partial, scale = lax.optimization_barrier((partial, scale))
    partial = partial.reshape(len(group), quarter, -1)
    columns = out_proj.shape[1]
    blocks = [None] * n_ctx
    for i, r in enumerate(group):
        block = partial[i] if r == 0 else swap(partial[i], "ctx", r)
        blocks[r] = block[:, :columns]
        blocks[r ^ 2] = block[:, columns:]
    stacked = jnp.stack(blocks)
    mixed = jnp.concatenate(
        [lax.dynamic_index_in_dim(stacked, me_ctx ^ b, 0, False) for b in range(n_ctx)], axis=1
    )
    return mixed.astype(F32), scale


def pack_kernel(*refs):
    out = refs[-1]
    row = 0
    for piece in refs[:-1]:
        rows = piece.shape[0]
        out[row : row + rows, :] = piece[...]
        row += rows


def pack(pieces):
    rows = sum(p.shape[0] for p in pieces)
    width = pieces[0].shape[1]
    whole = pl.BlockSpec(memory_space=pltpu.VMEM)
    return pl.pallas_call(
        pack_kernel,
        out_shape=jax.ShapeDtypeStruct((rows, width), pieces[0].dtype),
        in_specs=[whole] * len(pieces),
        out_specs=whole,
        compiler_params=pltpu.CompilerParams(vmem_limit_bytes=32 * 1024 * 1024),
        cost_estimate=pl.CostEstimate(flops=0, bytes_accessed=4 * rows * width, transcendentals=0),
    )(*pieces)


def expert_kernel(
    own, mate, gate, up, down, pick, out_own, out_mate, rows, hidden, gu, dn, row_sem, gu_sem, dn_sem
):
    half = own.shape[0]
    model = gate.shape[0]
    tiles = gate.shape[1] // LANES
    down_tiles = model // DOWN_TILE
    row_copies = [
        pltpu.make_async_copy(own, rows.at[pl.ds(0, half)], row_sem.at[0]),
        pltpu.make_async_copy(mate, rows.at[pl.ds(half, half)], row_sem.at[1]),
    ]

    def gu_copies(j):
        at = pl.ds(pl.multiple_of(j * LANES, LANES), LANES)
        s = lax.rem(j, GU_SLOTS)
        return [
            pltpu.make_async_copy(gate.at[:, at], gu.at[s, :, pl.ds(0, LANES)], gu_sem.at[s, 0]),
            pltpu.make_async_copy(up.at[:, at], gu.at[s, :, pl.ds(LANES, LANES)], gu_sem.at[s, 1]),
        ]

    def dn_copy(j):
        at = pl.ds(pl.multiple_of(j * DOWN_TILE, DOWN_TILE), DOWN_TILE)
        s = lax.rem(j, DN_SLOTS)
        return pltpu.make_async_copy(down.at[:, at], dn.at[s], dn_sem.at[s])

    for c in row_copies:
        c.start()
    for j in range(GU_SLOTS - 1):
        for c in gu_copies(j):
            c.start()
    for c in row_copies:
        c.wait()

    def gate_up(j, carry):
        ahead = j + GU_SLOTS - 1
        for c in gu_copies(j):
            c.wait()

        @pl.when(ahead < tiles)
        def _():
            for c in gu_copies(ahead):
                c.start()

        @pl.when((ahead >= tiles) & (ahead - tiles < DN_SLOTS - 1))
        def _():
            dn_copy(ahead - tiles).start()

        both = mm(rows[:, :model], gu[lax.rem(j, GU_SLOTS)])
        gate_val = both[:, :LANES]
        act = gate_val / (1.0 + jnp.exp(-gate_val)) * both[:, LANES:]
        hidden[:, pl.ds(pl.multiple_of(j * LANES, LANES), LANES)] = act.astype(BF)
        return carry

    lax.fori_loop(0, tiles, gate_up, 0)
    weight = jnp.sum(rows[:, model:].astype(F32) * pick[...], axis=1, keepdims=True)

    def down_part(j, carry):
        dn_copy(j).wait()

        @pl.when(j + DN_SLOTS - 1 < down_tiles)
        def _():
            dn_copy(j + DN_SLOTS - 1).start()

        part = mm(hidden[...], dn[lax.rem(j, DN_SLOTS)]) * weight
        at = pl.ds(pl.multiple_of(j * DOWN_TILE, DOWN_TILE), DOWN_TILE)
        out_own[:, at] = part[:half].astype(BF)
        out_mate[:, at] = part[half:].astype(BF)
        return carry

    lax.fori_loop(0, down_tiles, down_part, 0)


def experts(own, mate, gate, up, down, pick):
    half, width = own.shape
    model, units = gate.shape
    out = jax.ShapeDtypeStruct((half, model), BF)
    whole = pl.BlockSpec(memory_space=pltpu.VMEM)
    anywhere = pl.BlockSpec(memory_space=pl.ANY)
    hbm = pl.BlockSpec(memory_space=pltpu.HBM)
    flops = 2 * 2 * half * model * units * 3
    moved = 2 * (3 * model * units + 8 * half * model)
    return pl.pallas_call(
        expert_kernel,
        out_shape=(out, out),
        in_specs=[anywhere] * 2 + [hbm] * 3 + [whole],
        out_specs=(whole, whole),
        scratch_shapes=[
            pltpu.VMEM((2 * half, width), BF),
            pltpu.VMEM((2 * half, units), BF),
            pltpu.VMEM((GU_SLOTS, model, 2 * LANES), BF),
            pltpu.VMEM((DN_SLOTS, units, DOWN_TILE), BF),
            pltpu.SemaphoreType.DMA((2,)),
            pltpu.SemaphoreType.DMA((GU_SLOTS, 2)),
            pltpu.SemaphoreType.DMA((DN_SLOTS,)),
        ],
        compiler_params=pltpu.CompilerParams(vmem_limit_bytes=48 * 1024 * 1024),
        cost_estimate=pl.CostEstimate(flops=flops, bytes_accessed=moved, transcendentals=2 * half * units),
    )(own, mate, gate, up, down, pick)


def together(values, others):
    return lax.optimization_barrier((tuple(values), others))


def across(x):
    n_ctx, n_exp = lax.axis_size("ctx"), lax.axis_size("exp")
    pairs = [
        (c * n_exp + e, (c ^ 1) * n_exp + (e ^ 2)) for c in range(n_ctx) for e in range(n_exp)
    ]
    return lax.ppermute(x, ("ctx", "exp"), pairs)


def summed(own, got, first, rows):
    last = first + rows
    return own[first:last].astype(F32) + got[first:last].astype(F32)


def plane_sums(own, got, others):
    size = own.shape[0] // 4
    sums = [summed(own, got, k * size, size).astype(BF) for k in (1, 2, 3)]
    (to_x,), others = together(sums[:1], others)
    return (swap(to_x, "exp", 2), swap(sums[1], "ctx", 1), across(sums[2])), others


def local(
    inputs,
    gate_input,
    b_proj,
    c_proj,
    step_size,
    decay_rate,
    skip_gain,
    start_state,
    norm_gain,
    out_proj,
    residual,
    moe_gain,
    w_gate,
    w_up,
    w_down,
    route_ids,
    route_gates,
):
    n_ctx = lax.axis_size("ctx")
    n_exp = lax.axis_size("exp")
    me_ctx = lax.axis_index("ctx")
    me_exp = lax.axis_index("exp")
    tok = inputs.shape[0]
    quarter = tok // n_exp
    pairs = n_ctx // 2
    named = route_ids[:, :, None] == jnp.arange(LANES // 2, dtype=jnp.int32)[None, None, :]
    weights = jnp.sum(jnp.where(named, route_gates[:, :, None], 0.0), axis=1)
    weights = lax.dynamic_slice_in_dim(weights, me_exp * quarter, quarter, 0)
    weights_high = weights.astype(BF)
    weights_low = (weights - weights_high.astype(F32)).astype(BF)
    lane = jnp.arange(LANES, dtype=jnp.int32)
    pick = (lane % (LANES // 2) == me_ctx // PAIR).astype(F32)[None, :]

    cut = out_proj.shape[0] // 8 * 3
    two_parts = (swap(out_proj[:cut], "ctx", 2), out_proj[cut:])
    gated, (first_part, second_part) = mixer_rows(
        inputs, gate_input, b_proj, c_proj, step_size, decay_rate, skip_gain, start_state, two_parts
    )
    neighbour_proj = jnp.concatenate([first_part, swap(second_part, "ctx", 2)])
    mixed, scale = project_rows(gated, norm_gain, out_proj, neighbour_proj)
    own_residual = lax.dynamic_slice_in_dim(residual, me_exp * quarter, quarter, 0)
    hidden = own_residual.astype(F32) + mixed * scale[:, None]
    moe_scale = lax.rsqrt(jnp.mean(hidden * hidden, axis=1, keepdims=True) + eps_norm)
    moe_in = (hidden * moe_scale * moe_gain[None, :]).astype(BF)

    payload = jnp.concatenate([moe_in, weights_high, weights_low], axis=1)
    order = [0] + list(range(2, pairs)) + [1]
    count = len(order)
    by_distance = [payload]
    for d in range(1, pairs):
        low = d & -d
        by_distance.append(swap(by_distance[d - low], "ctx", 2 * low))
    planes = [by_distance[d] for d in order]
    near, rows, results, got, far_got, parts = [], [], [], [], [], []

    def sides(k):
        return (("ctx", 1), ("exp", 2)) if k < count - 2 else (("exp", 2), ("ctx", 1))

    def in_steps(k):
        return k < count - 1

    def bring(k):
        if k < min(count, 3):
            one, two = sides(k)
            near.append((swap(planes[k], *one), swap(planes[k], *two), across(planes[k])))

    def bring_first(k):
        if 3 <= k < count:
            near.append((swap(planes[k], *sides(k)[0]),))

    def bring_second(k):
        if 3 <= k < count:
            near[k] = (*near[k], swap(pack((planes[k], *near[k])), *sides(k)[1]))

    def ready(k):
        own = pack((planes[k], *near[k]))
        rows.append((own, swap(own, "exp", 1)))

    def core(k):
        if 0 <= k < count:
            got.append(swap(results[k][1], "exp", 1))

    def spread(k):
        if 0 <= k < count:
            own = results[k][0]
            if in_steps(k):
                half = own.shape[0] // 2
                far_got.append((swap(summed(own, got[k], half, half).astype(BF), *sides(k)[1]),))
            else:
                last, far_got[1:] = plane_sums(own, got[k], far_got[1:])
                far_got.append(last)

    def spread_second(k):
        if 0 <= k < count and len(far_got[k]) == 1:
            first = far_got[k][0]
            size = first.shape[0] // 2
            second = summed(results[k][0], got[k], size, size) + first[size:].astype(F32)
            far_got[k] = (first, swap(second.astype(BF), *sides(k)[0]))

    def back(k):
        if 0 <= k < count:
            part = summed(results[k][0], got[k], 0, quarter)
            for v in far_got[k]:
                part = part + v[:quarter].astype(F32)
            d = order[k]
            parts.append(part if d == 0 else swap(part.astype(BF), "ctx", 2 * d))

    def sums(stage):
        core(stage - 1)
        if stage - 2 < count - 2:
            spread(stage - 2)
        spread_second(stage - 3)
        if stage == count - 1:
            spread(count - 2)
        if stage == count:
            spread_second(count - 2)
            spread(count - 1)
        back(stage - 4)

    bring(0)
    near[0], planes[1] = together(near[0], planes[1])
    for i in range(count):
        ready(i)
        sums(i)
        bring(i + 1)
        bring_second(i + 1)
        if i > 0:
            bring_first(i + 2)
        beside = (got[-1:], far_got[: count - 2], parts[-1:], near[i + 1 : i + 2], planes[i + 2 :])
        results.append(experts(*rows[i], w_gate[0], w_up[0], w_down[0], pick))
        results[i], beside = together(results[i], beside)
        got[-1:], far_got[: count - 2], parts[-1:], near[i + 1 : i + 2], planes[i + 2 :] = beside
    for i in range(count, count + 4):
        sums(i)
    for part in parts:
        hidden = hidden + part.astype(F32)
    return hidden.astype(BF)


def solution(mesh):
    in_specs = (
        P("ctx", "exp"),
        P("ctx", "exp"),
        P("ctx", None),
        P("ctx", None),
        P("exp", "ctx"),
        P("exp", "ctx"),
        P("exp"),
        P("exp", None, None),
        P("exp"),
        P("exp", "ctx"),
        P("ctx", None),
        P(),
        P("ctx", None, "exp"),
        P("ctx", None, "exp"),
        P("ctx", "exp", None),
        P("ctx", None),
        P("ctx", None),
    )
    out_specs = P(("ctx", "exp"), None)
    return jax.shard_map(local, mesh=mesh, in_specs=in_specs, out_specs=out_specs, check_vma=False)
```
